32 devices in a mesh: dp: 8 (over z, x), fsdp: 4 (over y, core).
Axes of the slice: x: 2, y: 2, z: 4, core: 2. Of those that a mesh axis runs over, the one named last changes fastest.
Arguments:
- tokens: bfloat16 [73728, 640], P(('dp', 'fsdp')), may hold values from -6 to 6
- cotangent: bfloat16 [73728, 640], P(('dp', 'fsdp')), may hold values from -6 to 6
- lengths: int32 [64, 4], P(('dp', 'fsdp')), may hold values from 1 to 1024, 1152 in all within a row
- w_query: bfloat16 [640, 1024], P(None, ('dp', 'fsdp')), may hold values from -0.25 to 0.25
- w_key: bfloat16 [640, 256], P(None, ('dp', 'fsdp')), may hold values from -0.25 to 0.25
- w_value: bfloat16 [640, 256], P(None, ('dp', 'fsdp')), may hold values from -0.25 to 0.25
- w_out: bfloat16 [1024, 640], P(('dp', 'fsdp')), may hold values from -0.1875 to 0.1875
- w_gate: bfloat16 [640, 2048], P(None, ('dp', 'fsdp')), may hold values from -0.25 to 0.25
- w_up: bfloat16 [640, 2048], P(None, ('dp', 'fsdp')), may hold values from -0.25 to 0.25
- w_down: bfloat16 [2048, 640], P(('dp', 'fsdp')), may hold values from -0.125 to 0.125
- gain_pre_attn: float32 [640], replicated, may hold values from 0.25 to 1.75
- gain_query: float32 [256], replicated, may hold values from 0.25 to 1.75
- gain_key: float32 [256], replicated, may hold values from 0.25 to 1.75
- gain_post_attn: float32 [640], replicated, may hold values from 0.25 to 1.75
- gain_pre_ff: float32 [640], replicated, may hold values from 0.25 to 1.75
- gain_post_ff: float32 [640], replicated, may hold values from 0.25 to 1.75
Outputs:
- layer_out: bfloat16 [73728, 640], P(('dp', 'fsdp'))
- grad_tokens: float32 [73728, 640], P(('dp', 'fsdp'))
- grad_query: float32 [640, 1024], P(None, ('dp', 'fsdp'))
- grad_key: float32 [640, 256], P(None, ('dp', 'fsdp'))
- grad_value: float32 [640, 256], P(None, ('dp', 'fsdp'))
- grad_out: float32 [1024, 640], P(('dp', 'fsdp'))
- grad_gate: float32 [640, 2048], P(None, ('dp', 'fsdp'))
- grad_up: float32 [640, 2048], P(None, ('dp', 'fsdp'))
- grad_down: float32 [2048, 640], P(('dp', 'fsdp'))
- grad_pre_attn: float32 [640], replicated
- grad_gain_query: float32 [256], replicated
- grad_gain_key: float32 [256], replicated
- grad_post_attn: float32 [640], replicated
- grad_pre_ff: float32 [640], replicated
- grad_post_ff: float32 [640], replicated
The draws below stay inside these ranges and needn't reach their ends.
Inputs may be any that keep to these rules, and one draw needn't show every extreme that they name: Each micro-batch's 4 lengths sum to 1152, and its longest document has exactly 1024 tokens.
All inputs are finite; a program needn't handle non-finite values.
Results may differ from the reference program's by a relative error of at most 0.017.
Values may be sent and summed in bfloat16 or wider, within the bound.
No kernel may reach another device: no remote copies, remote signals or barrier semaphores. Data moves between devices by JAX's collectives and lax.ppermute only.
A program may use at most 256 MiB of HBM per device.

```python
import math
import jax
import jax.numpy as jnp
import numpy as np
from jax import lax

D = 640
HQ = 4
HD = 256
FF = 2048
WINDOW = 512
ROW = 1152
LONGEST = 1024
DOCS = 4
TOKENS = 73728
BATCHES = 64


def block_levels(stream_key, extent, shards, least, largest):
    gain, own = 1.0, jax.random.fold_in(stream_key, 6)
    for dim, parts in shards:
        steps = jnp.exp(jax.random.uniform(jax.random.fold_in(own, dim), (parts,), jnp.float32, least / len(shards), largest / len(shards)))
        gain = gain * jnp.repeat(steps, extent[dim] // parts).reshape([-1 if axis == dim else 1 for axis in range(len(extent))])
    return gain


def split_up(count, total, most, skew):
    portions = [(1 << 20) // math.isqrt(grade ** skew) + 1 for grade in range(2, count + 1)]
    surplus, holding = total - most - (count - 1), [1] * (count - 1)
    while surplus > 0:
        movable = [i for i in range(count - 1) if holding[i] < most]
        pool, remaining = sum([portions[i] for i in movable]), surplus
        for i in movable:
            more = min(most - holding[i], max(1, remaining * portions[i] // pool), surplus)
            holding[i] = holding[i] + more
            surplus = surplus - more
    return np.array([most] + holding)


def uneven(own_key, number_of, total, bound, skew):
    if number_of == 2:
        one = jax.random.randint(own_key, (), max(1, total - bound), min(bound, total - 1) + 1)
        return jnp.stack([one, total - one])
    tallies = jnp.asarray(split_up(number_of, total, bound, skew), jnp.int32)
    twos = (number_of - 1) // 2
    source_of, sink = tallies[1:1 + 2 * twos:2], tallies[2:2 + 2 * twos:2]
    margin = jnp.minimum(source_of - 1, bound - sink)
    shifted = jax.random.randint(jax.random.fold_in(own_key, 1), (twos,), 0, 1 << 20) % (margin + 1)
    tallies = tallies.at[1:1 + 2 * twos:2].set(source_of - shifted).at[2:2 + 2 * twos:2].set(sink + shifted)
    return tallies[jax.random.permutation(jax.random.fold_in(own_key, 2), number_of)]


def scatter_about(rng, extent, scale, most, cuts=(), held_as=jnp.bfloat16):
    array = jax.random.normal(rng, extent, jnp.float32) * scale
    if len(cuts) > 0:
        array = block_levels(rng, extent, cuts, -0.22, 0.18) * array
    return jnp.clip(array, min=-most, max=most).astype(held_as)


def setup_inputs(seed: int = 0) -> dict:
    streams_of = jax.random.split(jax.random.key(seed), 17)
    return {
        "tokens": scatter_about(streams_of[0], (TOKENS, D), 1.0, 6.0, ((0, 32),)),
        "cotangent": scatter_about(streams_of[1], (TOKENS, D), 1.0, 6.0, ((0, 32),)),
        "lengths": jax.vmap(lambda own: uneven(own, DOCS, ROW, LONGEST, 2))(jax.random.split(streams_of[2], BATCHES)).reshape((BATCHES, DOCS)).astype(jnp.int32),
        "w_query": scatter_about(streams_of[3], (D, HQ * HD), D ** -0.5, 0.25, ((1, 32),)),
        "w_key": scatter_about(streams_of[4], (D, HD), D ** -0.5, 0.25, ((1, 32),)),
        "w_value": scatter_about(streams_of[5], (D, HD), D ** -0.5, 0.25, ((1, 32),)),
        "w_out": scatter_about(streams_of[6], (HQ * HD, D), (HQ * HD) ** -0.5, 0.1875, ((0, 32),)),
        "w_gate": scatter_about(streams_of[7], (D, FF), D ** -0.5, 0.25, ((1, 32),)),
        "w_up": scatter_about(streams_of[8], (D, FF), D ** -0.5, 0.25, ((1, 32),)),
        "w_down": scatter_about(streams_of[9], (FF, D), FF ** -0.5, 0.125, ((0, 32),)),
        "gain_pre_attn": jnp.clip(1.0 + 0.15 * jax.random.normal(streams_of[10], (D,), jnp.float32), 0.25, 1.75),
        "gain_query": jnp.clip(1.0 + 0.15 * jax.random.normal(streams_of[11], (HD,), jnp.float32), 0.25, 1.75),
        "gain_key": jnp.clip(1.0 + 0.15 * jax.random.normal(streams_of[12], (HD,), jnp.float32), 0.25, 1.75),
        "gain_post_attn": jnp.clip(1.0 + 0.15 * jax.random.normal(streams_of[13], (D,), jnp.float32), 0.25, 1.75),
        "gain_pre_ff": jnp.clip(1.0 + 0.15 * jax.random.normal(streams_of[14], (D,), jnp.float32), 0.25, 1.75),
        "gain_post_ff": jnp.clip(1.0 + 0.15 * jax.random.normal(streams_of[15], (D,), jnp.float32), 0.25, 1.75),
    }


@jax.custom_vjp
def low(v):
    return lax.optimization_barrier(v.astype(jnp.bfloat16)).astype(jnp.float32)

@jax.custom_vjp
def low_back(v):
    return v

def low_keep(v):
    return (low(v), None)

def low_pass(kept, grad):
    return (grad,)

def back_keep(v):
    return (v, None)

def back_low(kept, grad):
    return (low(grad),)
low.defvjp(low_keep, low_pass)
low_back.defvjp(back_keep, back_low)
epsilon = 1e-06
highest = lax.Precision.HIGHEST

def matmul(left, right):
    return jnp.dot(left, right, precision=highest, preferred_element_type=jnp.float32)

def rms_scale(values, scale_gain):
    return values * lax.rsqrt(lax.optimization_barrier(jnp.mean(values * values, axis=-1, keepdims=True)) + epsilon) * scale_gain

def rotate(values, angles):
    half_size = values.shape[-1] // 2
    cos_part = jnp.cos(angles)[:, None, :]
    sin_part = jnp.sin(angles)[:, None, :]
    leading = values[..., :half_size]
    trailing = values[..., half_size:]
    return jnp.concatenate([leading * cos_part - trailing * sin_part, trailing * cos_part + leading * sin_part], axis=-1)

def layout(doc_lengths, row_count, window_size, head_size):
    places = jnp.arange(row_count, dtype=jnp.int32)
    doc_ends = jnp.cumsum(doc_lengths.astype(jnp.int32)).astype(jnp.int32)
    passed = places[:, None] >= doc_ends[None, :]
    doc_index = lax.optimization_barrier(jnp.sum(passed.astype(jnp.int32), axis=1)).astype(jnp.int32)
    doc_start = lax.optimization_barrier(jnp.sum(jnp.where(passed, doc_lengths[None, :].astype(jnp.int32), 0), axis=1)).astype(jnp.int32)
    position = (places - doc_start).astype(jnp.float32)
    steps_back = places[:, None] - places[None, :]
    visible = (doc_index[:, None] == doc_index[None, :]) & (steps_back >= 0) & (steps_back < window_size)
    frequency = jnp.exp(jnp.arange(head_size // 2, dtype=jnp.float32) * (-2.0 * math.log(10000.0) / head_size))
    angles = position[:, None] * frequency[None, :]
    return (angles, visible)

def block_forward(source, weights, gains, angles, visible):
    w_query, w_key, w_value, w_out, w_gate, w_up, w_down = weights
    gain_pre_attn, gain_query, gain_key, gain_post_attn, gain_pre_ff, gain_post_ff = gains
    row_count = source.shape[0]
    normed = low(rms_scale(source, gain_pre_attn))
    query_raw = low_back(matmul(normed, w_query)).reshape(row_count, HQ, HD)
    key_raw = low_back(matmul(normed, w_key))
    value_rows = low(low_back(matmul(normed, w_value)))
    queries = low(rotate(rms_scale(query_raw, gain_query), angles))
    keys_rot = low(rotate(rms_scale(key_raw[:, None, :], gain_key), angles))[:, 0, :]
    scores = low_back(jnp.einsum('rhd,cd->hrc', queries, keys_rot, precision=highest) * HD ** (-0.5))
    scores = jnp.where(visible[None], scores, -1e+30)
    row_max = lax.optimization_barrier(jnp.max(scores, axis=-1, keepdims=True))
    exponent = jnp.exp(scores - row_max)
    attention = low(exponent / lax.optimization_barrier(jnp.sum(exponent, axis=-1, keepdims=True)))
    context = low(low_back(jnp.einsum('hrc,cd->rhd', attention, value_rows, precision=highest))).reshape(row_count, HQ * HD)
    branch = low_back(matmul(context, w_out))
    middle = source + rms_scale(branch, gain_post_attn)
    normed_ff = low(rms_scale(middle, gain_pre_ff))
    gate_pre = low_back(matmul(normed_ff, w_gate))
    up_pre = low_back(matmul(normed_ff, w_up))
    hidden = low(jax.nn.gelu(gate_pre, approximate=True) * up_pre)
    down_out = low_back(matmul(hidden, w_down))
    return middle + rms_scale(down_out, gain_post_ff)

def reference(tokens, cotangent, lengths, w_query, w_key, w_value, w_out, w_gate, w_up, w_down, gain_pre_attn, gain_query, gain_key, gain_post_attn, gain_pre_ff, gain_post_ff):
    weights = tuple((matrix.astype(jnp.float32) for matrix in (w_query, w_key, w_value, w_out, w_gate, w_up, w_down)))
    gains = (gain_pre_attn, gain_query, gain_key, gain_post_attn, gain_pre_ff, gain_post_ff)
    row_total = lengths.shape[0]
    sources = tokens.astype(jnp.float32).reshape(row_total, ROW, D)
    cot_rows = cotangent.astype(jnp.float32).reshape(row_total, ROW, D)

    def row_step(running, inputs_row):
        source, cot_row, doc_lengths = inputs_row
        angles, visible = layout(doc_lengths, ROW, WINDOW, HD)
        result, backward = jax.vjp(lambda s, w, g: block_forward(s, w, g, angles, visible), source, weights, gains)
        grad_source, grad_weights, grad_gains = backward(cot_row)
        running = jax.tree.map(lambda a, b: a + b, running, (grad_weights, grad_gains))
        return (running, (result.astype(jnp.bfloat16), grad_source))
    start_sums = jax.tree.map(jnp.zeros_like, (weights, gains))
    sums, outputs = lax.scan(row_step, start_sums, (sources, cot_rows, lengths))
    grad_weights, grad_gains = sums
    results, grad_sources = outputs
    return (results.reshape(row_total * ROW, D), grad_sources.reshape(row_total * ROW, D), grad_weights[0], grad_weights[1], grad_weights[2], grad_weights[3], grad_weights[4], grad_weights[5], grad_weights[6], grad_gains[0], grad_gains[1], grad_gains[2], grad_gains[3], grad_gains[4], grad_gains[5])
```

```python
import functools
import math

import jax
import jax.numpy as jnp
from jax import lax
from jax.sharding import PartitionSpec as P

HQ = 4
HD = 256
WINDOW = 512
AXES = ("dp", "fsdp")
epsilon = 1e-06


def rms_scale(values, scale_gain):
    return (
        values * lax.rsqrt(jnp.mean(values * values, axis=-1, keepdims=True) + epsilon) * scale_gain
    )


def rotate(values, angles):
    half_size = values.shape[-1] // 2
    cos_part = jnp.cos(angles)[:, None, :]
    sin_part = jnp.sin(angles)[:, None, :]
    leading = values[..., :half_size]
    trailing = values[..., half_size:]
    return jnp.concatenate(
        [leading * cos_part - trailing * sin_part, trailing * cos_part + leading * sin_part],
        axis=-1,
    )


def layout(doc_lengths, row_count, window_size, head_size):
    places = jnp.arange(row_count, dtype=jnp.int32)
    doc_ends = jnp.cumsum(doc_lengths)
    passed = places[:, None] >= doc_ends[None, :]
    doc_index = jnp.sum(passed.astype(jnp.int32), axis=1)
    doc_start = jnp.sum(jnp.where(passed, doc_lengths[None, :], 0), axis=1)
    position = (places - doc_start).astype(jnp.float32)
    steps_back = places[:, None] - places[None, :]
    visible = (
        (doc_index[:, None] == doc_index[None, :]) & (steps_back >= 0) & (steps_back < window_size)
    )
    frequency = jnp.exp(
        jnp.arange(head_size // 2, dtype=jnp.float32) * (-2.0 * math.log(10000.0) / head_size)
    )
    angles = position[:, None] * frequency[None, :]
    return (angles, visible)


def head_prep(query_raw, key_raw, gain_query, gain_key, angles):
    row_count = query_raw.shape[0]
    queries = rotate(rms_scale(query_raw.reshape(row_count, HQ, HD), gain_query), angles)
    keys_rot = rotate(rms_scale(key_raw[:, None, :], gain_key), angles)[:, 0, :]
    return (queries, keys_rot)


def gelu_product(gate_pre, up_pre):
    return jax.nn.gelu(gate_pre, approximate=True) * up_pre


def product(form, left, right):
    return jnp.einsum(form, left, right, preferred_element_type=jnp.float32)


def swap(x, bit, count):
    return lax.ppermute(x, AXES, [(i, i ^ bit) for i in range(count)])


def bit_orders(count):
    bits = [1 << k for k in range(count.bit_length() - 1)]
    middle = bits[1:-1][::-1]
    orders = []
    for turn in range(3):
        turn %= max(len(middle), 1)
        orders.append([bits[-1]] + middle[turn:] + middle[:turn] + [bits[0]])
    return orders


def gather_relative(x, order, count):
    for bit in order:
        x = jnp.concatenate([x, swap(x, bit, count)], axis=0)
    return x


def gather_absolute(x, order, count, me):
    held = []
    for bit in order:
        other = swap(x, bit, count)
        mine_second = (me & bit) != 0
        axis = sum(1 for b in held if b > bit)
        x = jnp.stack(
            [jnp.where(mine_second, other, x), jnp.where(mine_second, x, other)], axis=axis
        )
        held.append(bit)
    return x.reshape((count,) + x.shape[len(order) :])


def places_of(order):
    count = 1 << len(order)
    return [sum(((m // bit) & 1) << k for k, bit in enumerate(order)) for m in range(count)]


def reorder(x, order_from, order_to, rows):
    n = len(order_from)
    y = x.reshape((2,) * n + (rows, x.shape[-1]))
    axes = [order_from[::-1].index(bit) for bit in order_to[::-1]]
    return y.transpose(axes + [n, n + 1]).reshape(x.shape)


def scatter_relative(x, order, count):
    for bit in order[::-1]:
        half = x.shape[0] // 2
        other = swap(x[half:], bit, count)
        total = x[:half].astype(jnp.float32) + other.astype(jnp.float32)
        x = total.astype(jnp.bfloat16) if bit != order[0] else total
    return x


def scatter_absolute(x, order, count, me):
    n = len(order)
    held = sorted(order)[::-1]
    x = x.reshape((2,) * n + x.shape[1:])
    for bit in order[::-1]:
        axis = held.index(bit)
        mine = ((me & bit) != 0).astype(jnp.int32)
        keep = lax.dynamic_index_in_dim(x, mine, axis, keepdims=False)
        send = lax.dynamic_index_in_dim(x, 1 - mine, axis, keepdims=False)
        held.remove(bit)
        total = keep.astype(jnp.float32) + swap(send, bit, count).astype(jnp.float32)
        x = total.astype(jnp.bfloat16) if bit != order[0] else total
    return x


def sum_everywhere(x, count):
    for k in range(count.bit_length() - 1):
        x = x + swap(x, 1 << k, count)
    return x


def body(
    tokens,
    cotangent,
    lengths,
    w_query,
    w_key,
    w_value,
    w_out,
    w_gate,
    w_up,
    w_down,
    gain_pre_attn,
    gain_query,
    gain_key,
    gain_post_attn,
    gain_pre_ff,
    gain_post_ff,
):
    micro_count = lengths.shape[0]
    row_count = tokens.shape[0] // micro_count
    width = tokens.shape[1]
    scale_factor = HD ** (-0.5)
    count = lax.axis_size(AXES)
    me = lax.axis_index(AXES)
    orders = bit_orders(count)
    q_rows, k_rows, o_rows, f_rows = (
        w_query.shape[1],
        w_key.shape[1],
        w_out.shape[0],
        w_gate.shape[1],
    )

    attn_shard = jnp.concatenate([w_query.T, w_key.T, w_value.T], axis=0)
    attn_all = gather_absolute(attn_shard, orders[0], count, me)
    full_query = attn_all[:, :q_rows].reshape(count * q_rows, width)
    full_key = attn_all[:, q_rows : q_rows + k_rows].reshape(count * k_rows, width)
    full_value = attn_all[:, q_rows + k_rows :].reshape(count * k_rows, width)
    full_out = gather_absolute(w_out, orders[1], count, me).reshape(count * o_rows, width)
    full_gate = gather_relative(w_gate.T, orders[0], count)
    full_up = reorder(gather_relative(w_up.T, orders[1], count), orders[1], orders[0], f_rows)
    full_down = reorder(gather_relative(w_down, orders[2], count), orders[2], orders[0], f_rows)

    source_f = tokens.astype(jnp.float32)
    upstream = cotangent.astype(jnp.float32)
    normed, back_pre_attn = jax.vjp(rms_scale, source_f, gain_pre_attn)
    normed_b = normed.astype(jnp.bfloat16)
    query_raw = product("rd,kd->rk", normed_b, full_query)
    key_raw = product("rd,kd->rk", normed_b, full_key)
    value_b = product("rd,kd->rk", normed_b, full_value).astype(jnp.bfloat16)

    kept = []
    contexts = []
    for m in range(micro_count):
        rows = slice(m * row_count, (m + 1) * row_count)
        angles, visible = layout(lengths[m], row_count, WINDOW, HD)
        (queries, keys_rot), back_heads = jax.vjp(
            lambda q, k, a, b: head_prep(q, k, a, b, angles),
            query_raw[rows],
            key_raw[rows],
            gain_query,
            gain_key,
        )
        queries_b = queries.astype(jnp.bfloat16)
        keys_b = keys_rot.astype(jnp.bfloat16)
        scores = product("rhd,cd->hrc", queries_b, keys_b) * scale_factor
        scores = jnp.where(visible[None], scores, -1e30)
        row_max = jnp.max(scores, axis=-1, keepdims=True)
        exponent = jnp.exp(scores - row_max)
        row_sum = jnp.sum(exponent, axis=-1, keepdims=True)
        attention_b = (exponent / row_sum).astype(jnp.bfloat16)
        context_b = product("hrc,cd->rhd", attention_b, value_b[rows]).astype(jnp.bfloat16)
        contexts.append(context_b.reshape(row_count, HQ * HD))
        kept.append((queries_b, keys_b, attention_b, back_heads))
    context_b = jnp.concatenate(contexts, axis=0)

    branch = product("rk,kd->rd", context_b, full_out)
    branch_normed, back_post_attn = jax.vjp(rms_scale, branch, gain_post_attn)
    middle = source_f + branch_normed
    normed_ff, back_pre_ff = jax.vjp(rms_scale, middle, gain_pre_ff)
    normed_ff_b = normed_ff.astype(jnp.bfloat16)
    gate_pre = product("rd,fd->rf", normed_ff_b, full_gate)
    up_pre = product("rd,fd->rf", normed_ff_b, full_up)
    hidden, back_gelu = jax.vjp(gelu_product, gate_pre, up_pre)
    hidden_b = hidden.astype(jnp.bfloat16)
    down_out = product("rf,fd->rd", hidden_b, full_down)
    down_normed, back_post_ff = jax.vjp(rms_scale, down_out, gain_post_ff)
    result = (middle + down_normed).astype(jnp.bfloat16)

    d_down, d_gain_post_ff = back_post_ff(upstream)
    d_down_b = d_down.astype(jnp.bfloat16)
    d_hidden = product("rd,fd->rf", d_down_b, full_down)
    d_gate, d_up = back_gelu(d_hidden)
    d_gate_b = d_gate.astype(jnp.bfloat16)
    d_up_b = d_up.astype(jnp.bfloat16)
    part_down = product("rf,rd->fd", hidden_b, d_down_b).astype(jnp.bfloat16)
    part_gate = product("rf,rd->fd", d_gate_b, normed_ff_b).astype(jnp.bfloat16)
    part_up = product("rf,rd->fd", d_up_b, normed_ff_b).astype(jnp.bfloat16)
    grad_gate = scatter_relative(part_gate, orders[0], count).T
    grad_up = scatter_relative(reorder(part_up, orders[0], orders[1], f_rows), orders[1], count).T
    grad_down = scatter_relative(reorder(part_down, orders[0], orders[2], f_rows), orders[2], count)

    d_normed_ff = product("rf,fd->rd", d_gate_b, full_gate) + product(
        "rf,fd->rd", d_up_b, full_up
    )
    d_middle_part, d_gain_pre_ff = back_pre_ff(d_normed_ff)
    d_middle = upstream + d_middle_part
    d_branch, d_gain_post_attn = back_post_attn(d_middle)
    d_branch_b = d_branch.astype(jnp.bfloat16)
    part_out = product("rk,rd->kd", context_b, d_branch_b).astype(jnp.bfloat16)
    grad_out = scatter_absolute(part_out.reshape(count, o_rows, width), orders[1], count, me)
    d_context_b = product("rd,kd->rk", d_branch_b, full_out).astype(jnp.bfloat16)

    d_query_parts, d_key_parts, d_value_parts = [], [], []
    d_gain_query = d_gain_key = 0.0
    for m in range(micro_count):
        rows = slice(m * row_count, (m + 1) * row_count)
        queries_b, keys_b, attention_b, back_heads = kept[m]
        d_context_m = d_context_b[rows].reshape(row_count, HQ, HD)
        attention_f = attention_b.astype(jnp.float32)
        d_attention = product("rhd,cd->hrc", d_context_m, value_b[rows])
        row_dot = jnp.sum(attention_f * d_attention, axis=-1, keepdims=True)
        d_scores_b = (attention_f * (d_attention - row_dot)).astype(jnp.bfloat16)
        d_queries = product("hrc,cd->rhd", d_scores_b, keys_b) * scale_factor
        d_keys = product("hrc,rhd->cd", d_scores_b, queries_b) * scale_factor
        d_value_b = product("hrc,rhd->cd", attention_b, d_context_m).astype(jnp.bfloat16)
        d_query_raw, d_key_raw, gq, gk = back_heads((d_queries, d_keys))
        d_gain_query += gq
        d_gain_key += gk
        d_query_parts.append(d_query_raw.astype(jnp.bfloat16))
        d_key_parts.append(d_key_raw.astype(jnp.bfloat16))
        d_value_parts.append(d_value_b)
    d_query_b = jnp.concatenate(d_query_parts, axis=0)
    d_key_b = jnp.concatenate(d_key_parts, axis=0)
    d_value_b = jnp.concatenate(d_value_parts, axis=0)
    part_query = product("rk,rd->kd", d_query_b, normed_b).astype(jnp.bfloat16)
    part_key = product("rk,rd->kd", d_key_b, normed_b).astype(jnp.bfloat16)
    part_value = product("rk,rd->kd", d_value_b, normed_b).astype(jnp.bfloat16)
    attn_part = jnp.concatenate(
        [
            part_query.reshape(count, q_rows, width),
            part_key.reshape(count, k_rows, width),
            part_value.reshape(count, k_rows, width),
        ],
        axis=1,
    )
    attn_grad = scatter_absolute(attn_part, orders[0], count, me)
    grad_query = attn_grad[:q_rows].T
    grad_key = attn_grad[q_rows : q_rows + k_rows].T
    grad_value = attn_grad[q_rows + k_rows :].T
    d_normed = (
        product("rk,kd->rd", d_query_b, full_query)
        + product("rk,kd->rd", d_key_b, full_key)
        + product("rk,kd->rd", d_value_b, full_value)
    )
    d_source_part, d_gain_pre_attn = back_pre_attn(d_normed)
    grad_source = d_middle + d_source_part

    gains = (
        d_gain_pre_attn,
        d_gain_query,
        d_gain_key,
        d_gain_post_attn,
        d_gain_pre_ff,
        d_gain_post_ff,
    )
    sizes = [g.shape[0] for g in gains]
    total = sum_everywhere(jnp.concatenate(gains).reshape(-1, 128), count).reshape(-1)
    gain_sums = []
    at = 0
    for size in sizes:
        gain_sums.append(total[at : at + size])
        at += size
    return (
        result,
        grad_source,
        grad_query,
        grad_key,
        grad_value,
        grad_out,
        grad_gate,
        grad_up,
        grad_down,
        *gain_sums,
    )


def solution(mesh):
    rows = P(("dp", "fsdp"), None)
    columns = P(None, ("dp", "fsdp"))
    return jax.shard_map(
        body,
        mesh=mesh,
        in_specs=(rows, rows, rows, columns, columns, columns, rows, columns, columns, rows)
        + (P(),) * 6,
        out_specs=(rows, rows, columns, columns, columns, rows, columns, columns, rows)
        + (P(),) * 6,
        check_vma=False,
    )
```

```python
import math

import jax
import jax.numpy as jnp
from jax import lax
from jax.experimental import pallas as pl
from jax.experimental.pallas import tpu as pltpu
from jax.sharding import PartitionSpec as P

HQ = 4
HD = 256
HALF = HD // 2
WINDOW = 512
AXES = ("dp", "fsdp")
EPS = 1e-06
SUB = 128
SPAN = WINDOW + SUB
TILE = 384
FF_TILE = 256
FF_CHUNK = 512
VMEM_LIMIT = 60 * 1024 * 1024
F32 = jnp.float32
BF16 = jnp.bfloat16
GELU_C = math.sqrt(2.0 / math.pi)


def dot(left, right):
    return lax.dot_general(left, right, (((1,), (0,)), ((), ())), preferred_element_type=F32)


def dot_t(left, right):
    return lax.dot_general(left, right, (((1,), (1,)), ((), ())), preferred_element_type=F32)


def row_mean(v):
    return jnp.mean(v, axis=-1, keepdims=True)


def norm_scale(v):
    return lax.rsqrt(row_mean(v * v) + EPS)


def norm_back(v, gain, upstream):
    r = norm_scale(v)
    unit = v * r
    gu = gain * upstream
    dv = r * (gu - unit * row_mean(unit * gu))
    return dv, jnp.sum(upstream * unit, axis=0, keepdims=True)


def stack_heads(x):
    return jnp.concatenate([x[:, h * HD : (h + 1) * HD] for h in range(HQ)], axis=0)


def turn(v, cos, sin):
    a, b = v[:, :HALF], v[:, HALF:]
    return jnp.concatenate([a * cos - b * sin, b * cos + a * sin], axis=1)


def turn_back(v, cos, sin):
    a, b = v[:, :HALF], v[:, HALF:]
    return jnp.concatenate([a * cos + b * sin, b * cos - a * sin], axis=1)


def attention_forward_kernel(
    low_ref,
    tok_ref,
    cos_ref,
    sin_ref,
    wq_ref,
    wk_ref,
    wv_ref,
    g_pre_ref,
    g_q_ref,
    g_k_ref,
    qraw_ref,
    kraw_ref,
    q_ref,
    k_ref,
    v_ref,
    prob_ref,
    ctx_ref,
):
    j = pl.program_id(1)

    @pl.when(j == 0)
    def _():
        k_ref[0, :WINDOW] = jnp.zeros((WINDOW, HD), BF16)
        v_ref[0, :WINDOW] = jnp.zeros((WINDOW, HD), BF16)

    x = tok_ref[...].astype(F32)
    normed = (x * norm_scale(x) * g_pre_ref[...]).astype(BF16)
    cos, sin = cos_ref[...], sin_ref[...]
    key_raw = dot_t(normed, wk_ref[...])
    kraw_ref[...] = key_raw
    here = pl.ds(pl.multiple_of(WINDOW + j * TILE, 128), TILE)
    k_ref[0, here] = turn(key_raw * norm_scale(key_raw) * g_k_ref[...], cos, sin).astype(BF16)
    v_ref[0, here] = dot_t(normed, wv_ref[...]).astype(BF16)
    for h in range(HQ):
        cols = slice(h * HD, (h + 1) * HD)
        raw = dot_t(normed, wq_ref[cols])
        qraw_ref[:, cols] = raw
        q_ref[:, cols] = turn(raw * norm_scale(raw) * g_q_ref[...], cos, sin).astype(BF16)
    for s in range(TILE // SUB):
        rows = slice(s * SUB, (s + 1) * SUB)
        first = j * TILE + s * SUB
        window = pl.ds(pl.multiple_of(first, 128), SPAN)
        queries = stack_heads(q_ref[rows]) * jnp.asarray(HD**-0.5, BF16)
        scores = dot_t(queries, k_ref[0, window])
        column = lax.broadcasted_iota(jnp.int32, (SUB, SPAN), 1) + (first - WINDOW)
        row = lax.broadcasted_iota(jnp.int32, (SUB, SPAN), 0) + first
        visible = (column >= low_ref[rows]) & (column <= row)
        scores = jnp.where(visible[None], scores.reshape(HQ, SUB, SPAN), -1e30)
        exponent = jnp.exp(scores - jnp.max(scores, axis=-1, keepdims=True))
        share = 1.0 / jnp.sum(exponent, axis=-1, keepdims=True)
        prob = (exponent * share).astype(BF16).reshape(HQ * SUB, SPAN)
        prob_ref[s] = prob
        context = dot(prob, v_ref[0, window]).astype(BF16)
        for h in range(HQ):
            ctx_ref[rows, h * HD : (h + 1) * HD] = context[h * SUB : (h + 1) * SUB]


def feed_forward_kernel(
    tok_ref,
    cot_ref,
    ctx_ref,
    wo_ref,
    gate_ref,
    up_ref,
    down_ref,
    g_attn_ref,
    g_pre_ref,
    g_post_ref,
    out_ref,
    d_mid_ref,
    d_ctx_ref,
    p_out_ref,
    p_gate_ref,
    p_up_ref,
    p_down_ref,
    d_g_attn_ref,
    d_g_pre_ref,
    d_g_post_ref,
    acc_out,
    acc_gate,
    acc_up,
    acc_down,
    hidden_sc,
    by_gate_sc,
    by_up_sc,
):
    step = pl.program_id(0)

    @pl.when(step == 0)
    def _():
        for ref in (acc_out, acc_gate, acc_up, acc_down, d_g_attn_ref, d_g_pre_ref, d_g_post_ref):
            ref[...] = jnp.zeros_like(ref)

    context = ctx_ref[...]
    branch = dot(context, wo_ref[...])
    middle = tok_ref[...].astype(F32) + branch * norm_scale(branch) * g_attn_ref[...]
    normed = (middle * norm_scale(middle) * g_pre_ref[...]).astype(BF16)
    units = gate_ref.shape[0]
    chunks = [slice(c, c + FF_CHUNK) for c in range(0, units, FF_CHUNK)]
    down_out = None
    for c in chunks:
        g = dot_t(normed, gate_ref[c])
        u = dot_t(normed, up_ref[c])
        g2 = g * g
        t = jnp.tanh(g * (GELU_C + (GELU_C * 0.044715) * g2))
        half = 0.5 * g
        gelu = half + half * t
        slope = (0.5 + 0.5 * t) + half * (1.0 - t * t) * (GELU_C + (3 * GELU_C * 0.044715) * g2)
        hidden = (gelu * u).astype(BF16)
        hidden_sc[:, c] = hidden
        by_gate_sc[:, c] = u * slope
        by_up_sc[:, c] = gelu
        part = dot(hidden, down_ref[c])
        down_out = part if down_out is None else down_out + part
    out_ref[...] = (middle + down_out * norm_scale(down_out) * g_post_ref[...]).astype(BF16)
    upstream = cot_ref[...].astype(F32)
    d_down, d_gain = norm_back(down_out, g_post_ref[...], upstream)
    d_g_post_ref[...] += d_gain
    d_down = d_down.astype(BF16)
    d_down_t = d_down.T
    normed_t = normed.T
    d_normed = None
    for c in chunks:
        d_hidden = dot_t(d_down, down_ref[c])
        d_gate = (d_hidden * by_gate_sc[:, c]).astype(BF16)
        d_up = (d_hidden * by_up_sc[:, c]).astype(BF16)
        acc_down[:, c] += dot(d_down_t, hidden_sc[:, c])
        acc_gate[:, c] += dot(normed_t, d_gate)
        acc_up[:, c] += dot(normed_t, d_up)
        part = dot(d_gate, gate_ref[c]) + dot(d_up, up_ref[c])
        d_normed = part if d_normed is None else d_normed + part
    d_middle, d_gain = norm_back(middle, g_pre_ref[...], d_normed)
    d_g_pre_ref[...] += d_gain
    d_middle = upstream + d_middle
    d_mid_ref[...] = d_middle
    d_branch, d_gain = norm_back(branch, g_attn_ref[...], d_middle)
    d_g_attn_ref[...] += d_gain
    d_branch = d_branch.astype(BF16)
    acc_out[...] += dot(d_branch.T, context)
    d_ctx_ref[...] = dot_t(d_branch, wo_ref[...]).astype(BF16)

    @pl.when(step == pl.num_programs(0) - 1)
    def _():
        for acc, ref in (
            (acc_out, p_out_ref),
            (acc_gate, p_gate_ref),
            (acc_up, p_up_ref),
            (acc_down, p_down_ref),
        ):
            for c in range(0, acc.shape[1], 256):
                ref[c : c + 256] = acc[:, c : c + 256].T.astype(BF16)


def attention_backward_kernel(
    tok_ref,
    d_mid_ref,
    d_ctx_ref,
    cos_ref,
    sin_ref,
    qraw_ref,
    kraw_ref,
    q_ref,
    k_ref,
    v_ref,
    prob_ref,
    wq_ref,
    wk_ref,
    wv_ref,
    g_pre_ref,
    g_q_ref,
    g_k_ref,
    d_tok_ref,
    p_q_ref,
    p_k_ref,
    p_v_ref,
    d_g_pre_ref,
    d_g_q_ref,
    d_g_k_ref,
    acc,
    d_keys,
    d_values,
    d_raw,
):
    batch, step = pl.program_id(0), pl.program_id(1)
    j = pl.num_programs(1) - 1 - step
    qcols = HQ * HD
    scale = HD**-0.5

    @pl.when((batch == 0) & (step == 0))
    def _():
        for ref in (acc, d_g_pre_ref, d_g_q_ref, d_g_k_ref):
            ref[...] = jnp.zeros_like(ref)

    @pl.when(step == 0)
    def _():
        d_keys[...] = jnp.zeros_like(d_keys)
        d_values[...] = jnp.zeros_like(d_values)

    for s in range(TILE // SUB):
        rows = slice(s * SUB, (s + 1) * SUB)
        window = pl.ds(pl.multiple_of(j * TILE + s * SUB, 128), SPAN)
        d_context = stack_heads(d_ctx_ref[rows])
        queries = stack_heads(q_ref[rows])
        keys, values = k_ref[0, window], v_ref[0, window]
        prob = prob_ref[s]
        d_prob = dot_t(d_context, values)
        weight = prob.astype(F32)
        row_dot = jnp.sum(weight * d_prob, axis=-1, keepdims=True)
        d_scores = (weight * (d_prob - row_dot)).astype(BF16)
        d_queries = dot(d_scores, keys) * scale
        d_keys[:, window] += dot(queries.T, d_scores)
        d_values[:, window] += dot(d_context.T, prob)
        cos, sin = cos_ref[rows], sin_ref[rows]
        for h in range(HQ):
            cols = slice(h * HD, (h + 1) * HD)
            back = turn_back(d_queries[h * SUB : (h + 1) * SUB], cos, sin)
            d_q, d_gain = norm_back(qraw_ref[rows, cols], g_q_ref[...], back)
            d_g_q_ref[...] += d_gain
            d_raw[rows, cols] = d_q.astype(BF16)
    here = pl.ds(pl.multiple_of(WINDOW + j * TILE, 128), TILE)
    back = turn_back(d_keys[:, here].T * scale, cos_ref[...], sin_ref[...])
    d_k, d_gain = norm_back(kraw_ref[...], g_k_ref[...], back)
    d_g_k_ref[...] += d_gain
    d_raw[:, qcols : qcols + HD] = d_k.astype(BF16)
    d_raw[:, qcols + HD :] = d_values[:, here].T.astype(BF16)

    x = tok_ref[...].astype(F32)
    normed = (x * norm_scale(x) * g_pre_ref[...]).astype(BF16)
    normed_t = normed.T
    for c in range(0, qcols + 2 * HD, 512):
        acc[:, c : c + 512] += dot(normed_t, d_raw[:, c : c + 512])
    d_normed = (
        dot(d_raw[:, :qcols], wq_ref[...])
        + dot(d_raw[:, qcols : qcols + HD], wk_ref[...])
        + dot(d_raw[:, qcols + HD :], wv_ref[...])
    )
    d_x, d_gain = norm_back(x, g_pre_ref[...], d_normed)
    d_g_pre_ref[...] += d_gain
    d_tok_ref[...] = d_mid_ref[...] + d_x

    @pl.when((batch == pl.num_programs(0) - 1) & (step == pl.num_programs(1) - 1))
    def _():
        for h in range(HQ):
            cols = slice(h * HD, (h + 1) * HD)
            p_q_ref[cols] = acc[:, cols].T.astype(BF16)
        p_k_ref[...] = acc[:, qcols : qcols + HD].T.astype(BF16)
        p_v_ref[...] = acc[:, qcols + HD :].T.astype(BF16)


def whole(shape):
    return pl.BlockSpec(shape, lambda *_: (0,) * len(shape), pipeline_mode=pl.Buffered(1))


def kept(shape):
    return pl.BlockSpec(shape, lambda *_: (0,) * len(shape))


def shape_of(shape, dtype=BF16):
    return jax.ShapeDtypeStruct(shape, dtype)


def attention_forward(tokens, low, cos, sin, wq, wk, wv, g_pre, g_q, g_k, batches):
    total, width = tokens.shape
    rows = total // batches
    steps = rows // TILE
    tile = lambda w: pl.BlockSpec((TILE, w), lambda b, j: (b * steps + j, 0))
    padded = pl.BlockSpec((1, WINDOW + rows, HD), lambda b, j: (b, 0, 0))
    subs = TILE // SUB
    flops = 2 * total * (width * (HQ + 2) * HD + 2 * HQ * HD * SPAN)
    return pl.pallas_call(
        attention_forward_kernel,
        grid=(batches, steps),
        in_specs=[
            tile(1),
            tile(width),
            tile(HALF),
            tile(HALF),
            whole(wq.shape),
            whole(wk.shape),
            whole(wv.shape),
            whole(g_pre.shape),
            whole(g_q.shape),
            whole(g_k.shape),
        ],
        out_specs=[
            tile(HQ * HD),
            tile(HD),
            tile(HQ * HD),
            padded,
            padded,
            pl.BlockSpec((subs, HQ * SUB, SPAN), lambda b, j: (b * steps + j, 0, 0)),
            tile(HQ * HD),
        ],
        out_shape=[
            shape_of((total, HQ * HD), F32),
            shape_of((total, HD), F32),
            shape_of((total, HQ * HD)),
            shape_of((batches, WINDOW + rows, HD)),
            shape_of((batches, WINDOW + rows, HD)),
            shape_of((total // SUB, HQ * SUB, SPAN)),
            shape_of((total, HQ * HD)),
        ],
        compiler_params=pltpu.CompilerParams(
            vmem_limit_bytes=VMEM_LIMIT, dimension_semantics=("arbitrary", "arbitrary")
        ),
        cost_estimate=pl.CostEstimate(
            flops=flops, bytes_accessed=30 << 20, transcendentals=total * HQ * SPAN
        ),
        name="attention_forward",
    )(low, tokens, cos, sin, wq, wk, wv, g_pre, g_q, g_k)


def feed_forward(tokens, cotangent, context, wo, gate, up, down, g_attn, g_pre, g_post):
    total, width = tokens.shape
    units = gate.shape[0]
    tile = lambda w: pl.BlockSpec((FF_TILE, w), lambda i: (i, 0))
    inner = context.shape[1]
    flops = 6 * total * width * (3 * units + inner)
    return pl.pallas_call(
        feed_forward_kernel,
        grid=(total // FF_TILE,),
        in_specs=[tile(width), tile(width), tile(inner)]
        + [whole(a.shape) for a in (wo, gate, up, down, g_attn, g_pre, g_post)],
        out_specs=[tile(width), tile(width), tile(inner)]
        + [whole(a.shape) for a in (wo, gate, up, down)]
        + [kept((1, width))] * 3,
        out_shape=[
            shape_of((total, width)),
            shape_of((total, width), F32),
            shape_of((total, inner)),
        ]
        + [shape_of(a.shape) for a in (wo, gate, up, down)]
        + [shape_of((1, width), F32)] * 3,
        scratch_shapes=[
            pltpu.VMEM((width, inner), F32),
            pltpu.VMEM((width, units), F32),
            pltpu.VMEM((width, units), F32),
            pltpu.VMEM((width, units), F32),
            pltpu.VMEM((FF_TILE, units), BF16),
            pltpu.VMEM((FF_TILE, units), F32),
            pltpu.VMEM((FF_TILE, units), F32),
        ],
        compiler_params=pltpu.CompilerParams(
            vmem_limit_bytes=VMEM_LIMIT, dimension_semantics=("arbitrary",)
        ),
        cost_estimate=pl.CostEstimate(
            flops=flops, bytes_accessed=40 << 20, transcendentals=total * units
        ),
        name="feed_forward",
    )(tokens, cotangent, context, wo, gate, up, down, g_attn, g_pre, g_post)


def attention_backward(
    tokens, d_middle, d_context, cos, sin, saved, wq, wk, wv, g_pre, g_q, g_k, batches
):
    total, width = tokens.shape
    rows = total // batches
    steps = rows // TILE
    back = lambda b, j: b * steps + steps - 1 - j
    tile = lambda w: pl.BlockSpec((TILE, w), lambda b, j: (back(b, j), 0))
    padded = pl.BlockSpec((1, WINDOW + rows, HD), lambda b, j: (b, 0, 0))
    subs = TILE // SUB
    columns = (HQ + 2) * HD
    flops = 2 * total * (width * columns * 2 + 4 * HQ * HD * SPAN)
    return pl.pallas_call(
        attention_backward_kernel,
        grid=(batches, steps),
        in_specs=[
            tile(width),
            tile(width),
            tile(HQ * HD),
            tile(HALF),
            tile(HALF),
            tile(HQ * HD),
            tile(HD),
            tile(HQ * HD),
            padded,
            padded,
            pl.BlockSpec((subs, HQ * SUB, SPAN), lambda b, j: (back(b, j), 0, 0)),
        ]
        + [whole(a.shape) for a in (wq, wk, wv, g_pre, g_q, g_k)],
        out_specs=[tile(width)]
        + [whole(a.shape) for a in (wq, wk, wv)]
        + [kept((1, width)), kept((1, HD)), kept((1, HD))],
        out_shape=[shape_of((total, width), F32)]
        + [shape_of(a.shape) for a in (wq, wk, wv)]
        + [shape_of((1, width), F32), shape_of((1, HD), F32), shape_of((1, HD), F32)],
        scratch_shapes=[
            pltpu.VMEM((width, columns), F32),
            pltpu.VMEM((HD, WINDOW + rows), F32),
            pltpu.VMEM((HD, WINDOW + rows), F32),
            pltpu.VMEM((TILE, columns), BF16),
        ],
        compiler_params=pltpu.CompilerParams(
            vmem_limit_bytes=VMEM_LIMIT, dimension_semantics=("arbitrary", "arbitrary")
        ),
        cost_estimate=pl.CostEstimate(flops=flops, bytes_accessed=45 << 20, transcendentals=0),
        name="attention_backward",
    )(tokens, d_middle, d_context, cos, sin, *saved, wq, wk, wv, g_pre, g_q, g_k)


def rows_layout(lengths, row_count):
    places = jnp.arange(row_count, dtype=jnp.int32)[None, :]
    ends = jnp.cumsum(lengths, axis=1)
    passed = places[:, :, None] >= ends[:, None, :]
    start = jnp.sum(jnp.where(passed, lengths[:, None, :], 0), axis=2)
    low = jnp.maximum(start, places - (WINDOW - 1)).reshape(-1, 1)
    frequency = jnp.exp(jnp.arange(HALF, dtype=F32) * (-2.0 * math.log(10000.0) / HD))
    angles = (places - start).astype(F32).reshape(-1, 1) * frequency[None, :]
    return low, jnp.cos(angles), jnp.sin(angles)


def swap(x, bit, count):
    return lax.ppermute(x, AXES, [(i, i ^ bit) for i in range(count)])


def bit_orders(count):
    bits = [1 << k for k in range(count.bit_length() - 1)]
    middle = bits[1:-1][::-1]
    orders = []
    for turn in range(3):
        turn %= max(len(middle), 1)
        orders.append([bits[-1]] + middle[turn:] + middle[:turn] + [bits[0]])
    return orders


def gather_relative(x, order, count):
    for bit in order:
        x = jnp.concatenate([x, swap(x, bit, count)], axis=0)
    return x


def gather_absolute(x, order, count, me):
    held = []
    for bit in order:
        other = swap(x, bit, count)
        mine_second = (me & bit) != 0
        axis = sum(1 for b in held if b > bit)
        x = jnp.stack(
            [jnp.where(mine_second, other, x), jnp.where(mine_second, x, other)], axis=axis
        )
        held.append(bit)
    return x.reshape((count,) + x.shape[len(order) :])


def places_of(order):
    count = 1 << len(order)
    return [sum(((m // bit) & 1) << k for k, bit in enumerate(order)) for m in range(count)]


def reorder(x, order_from, order_to, rows):
    n = len(order_from)
    y = x.reshape((2,) * n + (rows, x.shape[-1]))
    axes = [order_from[::-1].index(bit) for bit in order_to[::-1]]
    return y.transpose(axes + [n, n + 1]).reshape(x.shape)


def scatter_relative(x, order, count):
    for bit in order[::-1]:
        half = x.shape[0] // 2
        other = swap(x[half:], bit, count)
        total = x[:half].astype(F32) + other.astype(F32)
        x = total.astype(BF16) if bit != order[0] else total
    return x


def scatter_absolute(x, order, count, me):
    n = len(order)
    held = sorted(order)[::-1]
    x = x.reshape((2,) * n + x.shape[1:])
    for bit in order[::-1]:
        axis = held.index(bit)
        mine = ((me & bit) != 0).astype(jnp.int32)
        keep = lax.dynamic_index_in_dim(x, mine, axis, keepdims=False)
        send = lax.dynamic_index_in_dim(x, 1 - mine, axis, keepdims=False)
        held.remove(bit)
        total = keep.astype(F32) + swap(send, bit, count).astype(F32)
        x = total.astype(BF16) if bit != order[0] else total
    return x


def sum_everywhere(x, count):
    for k in range(count.bit_length() - 1):
        x = x + swap(x, 1 << k, count)
    return x


def body(
    tokens,
    cotangent,
    lengths,
    w_query,
    w_key,
    w_value,
    w_out,
    w_gate,
    w_up,
    w_down,
    gain_pre_attn,
    gain_query,
    gain_key,
    gain_post_attn,
    gain_pre_ff,
    gain_post_ff,
):
    batches = lengths.shape[0]
    row_count = tokens.shape[0] // batches
    width = tokens.shape[1]
    count = lax.axis_size(AXES)
    me = lax.axis_index(AXES)
    orders = bit_orders(count)
    q_rows, k_rows, o_rows, f_rows = (
        w_query.shape[1],
        w_key.shape[1],
        w_out.shape[0],
        w_gate.shape[1],
    )
    flat = lambda gain: gain.reshape(1, -1)

    attn_shard = jnp.concatenate([w_query.T, w_key.T, w_value.T], axis=0)
    attn_all = gather_absolute(attn_shard, orders[0], count, me)
    full_query = attn_all[:, :q_rows].reshape(count * q_rows, width)
    full_key = attn_all[:, q_rows : q_rows + k_rows].reshape(count * k_rows, width)
    full_value = attn_all[:, q_rows + k_rows :].reshape(count * k_rows, width)
    full_out = gather_absolute(w_out, orders[1], count, me).reshape(count * o_rows, width)
    full_gate = gather_relative(w_gate.T, orders[0], count)
    full_up = reorder(gather_relative(w_up.T, orders[1], count), orders[1], orders[0], f_rows)
    full_down = reorder(gather_relative(w_down, orders[2], count), orders[2], orders[0], f_rows)

    low, cos, sin = rows_layout(lengths, row_count)
    *saved, context = attention_forward(
        tokens,
        low,
        cos,
        sin,
        full_query,
        full_key,
        full_value,
        flat(gain_pre_attn),
        flat(gain_query),
        flat(gain_key),
        batches,
    )
    (
        result,
        d_middle,
        d_context,
        part_out,
        part_gate,
        part_up,
        part_down,
        d_gain_post_attn,
        d_gain_pre_ff,
        d_gain_post_ff,
    ) = feed_forward(
        tokens,
        cotangent,
        context,
        full_out,
        full_gate,
        full_up,
        full_down,
        flat(gain_post_attn),
        flat(gain_pre_ff),
        flat(gain_post_ff),
    )
    grad_gate = scatter_relative(part_gate, orders[0], count).T
    grad_up = scatter_relative(reorder(part_up, orders[0], orders[1], f_rows), orders[1], count).T
    grad_down = scatter_relative(reorder(part_down, orders[0], orders[2], f_rows), orders[2], count)
    grad_out = scatter_absolute(part_out.reshape(count, o_rows, width), orders[1], count, me)

    (
        grad_source,
        part_query,
        part_key,
        part_value,
        d_gain_pre_attn,
        d_gain_query,
        d_gain_key,
    ) = attention_backward(
        tokens,
        d_middle,
        d_context,
        cos,
        sin,
        saved,
        full_query,
        full_key,
        full_value,
        flat(gain_pre_attn),
        flat(gain_query),
        flat(gain_key),
        batches,
    )
    attn_part = jnp.concatenate(
        [
            part_query.reshape(count, q_rows, width),
            part_key.reshape(count, k_rows, width),
            part_value.reshape(count, k_rows, width),
        ],
        axis=1,
    )
    attn_grad = scatter_absolute(attn_part, orders[0], count, me)
    grad_query = attn_grad[:q_rows].T
    grad_key = attn_grad[q_rows : q_rows + k_rows].T
    grad_value = attn_grad[q_rows + k_rows :].T

    gains = (
        d_gain_pre_attn,
        d_gain_query,
        d_gain_key,
        d_gain_post_attn,
        d_gain_pre_ff,
        d_gain_post_ff,
    )
    total = sum_everywhere(jnp.concatenate(gains, axis=1).reshape(-1, 128), count).reshape(-1)
    gain_sums = []
    at = 0
    for gain in gains:
        gain_sums.append(total[at : at + gain.size])
        at += gain.size
    return (
        result,
        grad_source,
        grad_query,
        grad_key,
        grad_value,
        grad_out,
        grad_gate,
        grad_up,
        grad_down,
        *gain_sums,
    )


def solution(mesh):
    rows = P(("dp", "fsdp"), None)
    columns = P(None, ("dp", "fsdp"))
    return jax.shard_map(
        body,
        mesh=mesh,
        in_specs=(rows, rows, rows, columns, columns, columns, rows, columns, columns, rows)
        + (P(),) * 6,
        out_specs=(rows, rows, columns, columns, columns, rows, columns, columns, rows)
        + (P(),) * 6,
        check_vma=False,
    )
```

```python
import functools
import math

import jax
import jax.numpy as jnp
from jax import lax
from jax.experimental import pallas as pl
from jax.experimental.pallas import tpu as pltpu
from jax.sharding import PartitionSpec as P

HQ = 4
HD = 256
HALF = HD // 2
WINDOW = 512
AXES = ("dp", "fsdp")
EPS = 1e-06
SUB = 128
SPAN = WINDOW + SUB
TILE = 384
FF_TILE = 256
FF_CHUNK = 1024
VMEM_LIMIT = 60 * 1024 * 1024
F32 = jnp.float32
BF16 = jnp.bfloat16
GELU_C = math.sqrt(2.0 / math.pi)


def dot(left, right):
    return lax.dot_general(left, right, (((1,), (0,)), ((), ())), preferred_element_type=F32)


def dot_t(left, right):
    return lax.dot_general(left, right, (((1,), (1,)), ((), ())), preferred_element_type=F32)


def row_mean(v):
    return jnp.mean(v, axis=-1, keepdims=True)


def norm_scale(v):
    return lax.rsqrt(row_mean(v * v) + EPS)


def norm_back(v, gain, upstream):
    r = norm_scale(v)
    unit = v * r
    gu = gain * upstream
    dv = r * (gu - unit * row_mean(unit * gu))
    return dv, jnp.sum(upstream * unit, axis=0, keepdims=True)


def stack_heads(x):
    return jnp.concatenate([x[:, h * HD : (h + 1) * HD] for h in range(HQ)], axis=0)


def turn(v, cos, sin):
    a, b = v[:, :HALF], v[:, HALF:]
    return jnp.concatenate([a * cos - b * sin, b * cos + a * sin], axis=1)


def turn_back(v, cos, sin):
    a, b = v[:, :HALF], v[:, HALF:]
    return jnp.concatenate([a * cos + b * sin, b * cos - a * sin], axis=1)


def attention_forward_kernel(
    low_ref,
    tok_ref,
    cos_ref,
    sin_ref,
    wq_ref,
    wk_ref,
    wv_ref,
    g_pre_ref,
    g_q_ref,
    g_k_ref,
    qraw_ref,
    kraw_ref,
    q_ref,
    k_ref,
    v_ref,
    prob_ref,
    ctx_ref,
):
    j = pl.program_id(1)

    @pl.when(j == 0)
    def _():
        k_ref[0, :WINDOW] = jnp.zeros((WINDOW, HD), BF16)
        v_ref[0, :WINDOW] = jnp.zeros((WINDOW, HD), BF16)

    x = tok_ref[...].astype(F32)
    normed = (x * norm_scale(x) * g_pre_ref[...]).astype(BF16)
    cos, sin = cos_ref[...], sin_ref[...]
    key_raw = dot_t(normed, wk_ref[...])
    kraw_ref[...] = key_raw
    here = pl.ds(pl.multiple_of(WINDOW + j * TILE, 128), TILE)
    k_ref[0, here] = turn(key_raw * norm_scale(key_raw) * g_k_ref[...], cos, sin).astype(BF16)
    v_ref[0, here] = dot_t(normed, wv_ref[...]).astype(BF16)
    for h in range(HQ):
        cols = slice(h * HD, (h + 1) * HD)
        raw = dot_t(normed, wq_ref[cols])
        qraw_ref[:, cols] = raw
        q_ref[:, cols] = turn(raw * norm_scale(raw) * g_q_ref[...], cos, sin).astype(BF16)
    for s in range(TILE // SUB):
        rows = slice(s * SUB, (s + 1) * SUB)
        first = j * TILE + s * SUB
        window = pl.ds(pl.multiple_of(first, 128), SPAN)
        queries = stack_heads(q_ref[rows]) * jnp.asarray(HD**-0.5, BF16)
        scores = dot_t(queries, k_ref[0, window])
        column = lax.broadcasted_iota(jnp.int32, (SUB, SPAN), 1) + (first - WINDOW)
        row = lax.broadcasted_iota(jnp.int32, (SUB, SPAN), 0) + first
        visible = (column >= low_ref[rows]) & (column <= row)
        scores = jnp.where(visible[None], scores.reshape(HQ, SUB, SPAN), -1e30)
        exponent = jnp.exp(scores - jnp.max(scores, axis=-1, keepdims=True))
        share = 1.0 / jnp.sum(exponent, axis=-1, keepdims=True)
        prob = (exponent * share).astype(BF16).reshape(HQ * SUB, SPAN)
        prob_ref[s] = prob
        context = dot(prob, v_ref[0, window]).astype(BF16)
        for h in range(HQ):
            ctx_ref[rows, h * HD : (h + 1) * HD] = context[h * SUB : (h + 1) * SUB]


def feed_forward_kernel(
    places,
    tok_ref,
    cot_ref,
    ctx_ref,
    wo_ref,
    gate_ref,
    up_ref,
    down_ref,
    g_attn_ref,
    g_pre_ref,
    g_post_ref,
    out_ref,
    d_mid_ref,
    d_ctx_ref,
    p_out_ref,
    p_gate_keep,
    p_gate_send,
    p_up_keep,
    p_up_send,
    p_down_keep,
    p_down_send,
    d_g_attn_ref,
    d_g_pre_ref,
    d_g_post_ref,
    acc_out,
    acc_gate,
    acc_up,
    acc_down,
    hidden_sc,
    by_gate_sc,
    by_up_sc,
):
    step = pl.program_id(0)

    @pl.when(step == 0)
    def _():
        for ref in (acc_out, acc_gate, acc_up, acc_down, d_g_attn_ref, d_g_pre_ref, d_g_post_ref):
            ref[...] = jnp.zeros_like(ref)

    context = ctx_ref[...]
    branch = dot(context, wo_ref[...])
    middle = tok_ref[...].astype(F32) + branch * norm_scale(branch) * g_attn_ref[...]
    normed = (middle * norm_scale(middle) * g_pre_ref[...]).astype(BF16)
    units = gate_ref.shape[0]
    chunks = [slice(c, c + FF_CHUNK) for c in range(0, units, FF_CHUNK)]
    down_out = None
    for c in chunks:
        g = dot_t(normed, gate_ref[c])
        u = dot_t(normed, up_ref[c])
        g2 = g * g
        t = jnp.tanh(g * (GELU_C + (GELU_C * 0.044715) * g2))
        half = 0.5 * g
        gelu = half + half * t
        slope = (0.5 + 0.5 * t) + half * (1.0 - t * t) * (GELU_C + (3 * GELU_C * 0.044715) * g2)
        hidden = (gelu * u).astype(BF16)
        hidden_sc[:, c] = hidden
        by_gate_sc[:, c] = u * slope
        by_up_sc[:, c] = gelu
        part = dot(hidden, down_ref[c])
        down_out = part if down_out is None else down_out + part
    out_ref[...] = (middle + down_out * norm_scale(down_out) * g_post_ref[...]).astype(BF16)
    upstream = cot_ref[...].astype(F32)
    d_down, d_gain = norm_back(down_out, g_post_ref[...], upstream)
    d_g_post_ref[...] += d_gain
    d_down = d_down.astype(BF16)
    d_down_t = d_down.T
    normed_t = normed.T
    d_normed = None
    for c in chunks:
        d_hidden = dot_t(d_down, down_ref[c])
        d_gate = (d_hidden * by_gate_sc[:, c]).astype(BF16)
        d_up = (d_hidden * by_up_sc[:, c]).astype(BF16)
        acc_down[:, c] += dot(d_down_t, hidden_sc[:, c])
        acc_gate[:, c] += dot(normed_t, d_gate)
        acc_up[:, c] += dot(normed_t, d_up)
        part = dot(d_gate, gate_ref[c]) + dot(d_up, up_ref[c])
        d_normed = part if d_normed is None else d_normed + part
    d_middle, d_gain = norm_back(middle, g_pre_ref[...], d_normed)
    d_g_pre_ref[...] += d_gain
    d_middle = upstream + d_middle
    d_mid_ref[...] = d_middle
    d_branch, d_gain = norm_back(branch, g_attn_ref[...], d_middle)
    d_g_attn_ref[...] += d_gain
    d_branch = d_branch.astype(BF16)
    acc_out[...] += dot(d_branch.T, context)
    d_ctx_ref[...] = dot_t(d_branch, wo_ref[...]).astype(BF16)

    @pl.when(step == pl.num_programs(0) - 1)
    def _():
        for c in range(0, acc_out.shape[1], 256):
            p_out_ref[c : c + 256] = acc_out[:, c : c + 256].T.astype(BF16)
        blocks = len(places[0])
        size = acc_gate.shape[1] // blocks
        for acc, place, keep, send in (
            (acc_gate, places[0], p_gate_keep, p_gate_send),
            (acc_up, places[1], p_up_keep, p_up_send),
            (acc_down, places[2], p_down_keep, p_down_send),
        ):
            for c in range(0, acc.shape[1], 256):
                part = acc[:, c : c + 256].T.astype(BF16)
                for k in range(256 // size):
                    half, at = divmod(place[c // size + k], blocks // 2)
                    ref = send if half else keep
                    ref[at * size : (at + 1) * size] = part[k * size : (k + 1) * size]


def attention_backward_kernel(
    tok_ref,
    d_mid_ref,
    d_ctx_ref,
    cos_ref,
    sin_ref,
    qraw_ref,
    kraw_ref,
    q_ref,
    k_ref,
    v_ref,
    prob_ref,
    wq_ref,
    wk_ref,
    wv_ref,
    g_pre_ref,
    g_q_ref,
    g_k_ref,
    d_tok_ref,
    p_q_ref,
    p_k_ref,
    p_v_ref,
    d_g_pre_ref,
    d_g_q_ref,
    d_g_k_ref,
    acc,
    d_keys,
    d_values,
    d_raw,
):
    batch, step = pl.program_id(0), pl.program_id(1)
    j = pl.num_programs(1) - 1 - step
    qcols = HQ * HD
    scale = HD**-0.5

    @pl.when((batch == 0) & (step == 0))
    def _():
        for ref in (acc, d_g_pre_ref, d_g_q_ref, d_g_k_ref):
            ref[...] = jnp.zeros_like(ref)

    @pl.when(step == 0)
    def _():
        d_keys[...] = jnp.zeros_like(d_keys)
        d_values[...] = jnp.zeros_like(d_values)

    for s in range(TILE // SUB):
        rows = slice(s * SUB, (s + 1) * SUB)
        window = pl.ds(pl.multiple_of(j * TILE + s * SUB, 128), SPAN)
        d_context = stack_heads(d_ctx_ref[rows])
        queries = stack_heads(q_ref[rows])
        keys, values = k_ref[0, window], v_ref[0, window]
        prob = prob_ref[s]
        d_prob = dot_t(d_context, values)
        weight = prob.astype(F32)
        row_dot = jnp.sum(weight * d_prob, axis=-1, keepdims=True)
        d_scores = (weight * (d_prob - row_dot)).astype(BF16)
        d_queries = dot(d_scores, keys) * scale
        d_keys[:, window] += dot(queries.T, d_scores)
        d_values[:, window] += dot(d_context.T, prob)
        cos, sin = cos_ref[rows], sin_ref[rows]
        for h in range(HQ):
            cols = slice(h * HD, (h + 1) * HD)
            back = turn_back(d_queries[h * SUB : (h + 1) * SUB], cos, sin)
            d_q, d_gain = norm_back(qraw_ref[rows, cols], g_q_ref[...], back)
            d_g_q_ref[...] += d_gain
            d_raw[rows, cols] = d_q.astype(BF16)
    here = pl.ds(pl.multiple_of(WINDOW + j * TILE, 128), TILE)
    back = turn_back(d_keys[:, here].T * scale, cos_ref[...], sin_ref[...])
    d_k, d_gain = norm_back(kraw_ref[...], g_k_ref[...], back)
    d_g_k_ref[...] += d_gain
    d_raw[:, qcols : qcols + HD] = d_k.astype(BF16)
    d_raw[:, qcols + HD :] = d_values[:, here].T.astype(BF16)

    x = tok_ref[...].astype(F32)
    normed = (x * norm_scale(x) * g_pre_ref[...]).astype(BF16)
    normed_t = normed.T
    for c in range(0, qcols + 2 * HD, 512):
        acc[:, c : c + 512] += dot(normed_t, d_raw[:, c : c + 512])
    d_normed = (
        dot(d_raw[:, :qcols], wq_ref[...])
        + dot(d_raw[:, qcols : qcols + HD], wk_ref[...])
        + dot(d_raw[:, qcols + HD :], wv_ref[...])
    )
    d_x, d_gain = norm_back(x, g_pre_ref[...], d_normed)
    d_g_pre_ref[...] += d_gain
    d_tok_ref[...] = d_mid_ref[...] + d_x

    @pl.when((batch == pl.num_programs(0) - 1) & (step == pl.num_programs(1) - 1))
    def _():
        for h in range(HQ):
            cols = slice(h * HD, (h + 1) * HD)
            p_q_ref[cols] = acc[:, cols].T.astype(BF16)
        p_k_ref[...] = acc[:, qcols : qcols + HD].T.astype(BF16)
        p_v_ref[...] = acc[:, qcols + HD :].T.astype(BF16)


def whole(shape):
    return pl.BlockSpec(shape, lambda *_: (0,) * len(shape), pipeline_mode=pl.Buffered(1))


def kept(shape):
    return pl.BlockSpec(shape, lambda *_: (0,) * len(shape))


def shape_of(shape, dtype=BF16):
    return jax.ShapeDtypeStruct(shape, dtype)


def attention_forward(tokens, low, cos, sin, wq, wk, wv, g_pre, g_q, g_k, batches):
    total, width = tokens.shape
    rows = total // batches
    steps = rows // TILE
    tile = lambda w: pl.BlockSpec((TILE, w), lambda b, j: (b * steps + j, 0))
    padded = pl.BlockSpec((1, WINDOW + rows, HD), lambda b, j: (b, 0, 0))
    subs = TILE // SUB
    flops = 2 * total * (width * (HQ + 2) * HD + 2 * HQ * HD * SPAN)
    return pl.pallas_call(
        attention_forward_kernel,
        grid=(batches, steps),
        in_specs=[
            tile(1),
            tile(width),
            tile(HALF),
            tile(HALF),
            whole(wq.shape),
            whole(wk.shape),
            whole(wv.shape),
            whole(g_pre.shape),
            whole(g_q.shape),
            whole(g_k.shape),
        ],
        out_specs=[
            tile(HQ * HD),
            tile(HD),
            tile(HQ * HD),
            padded,
            padded,
            pl.BlockSpec((subs, HQ * SUB, SPAN), lambda b, j: (b * steps + j, 0, 0)),
            tile(HQ * HD),
        ],
        out_shape=[
            shape_of((total, HQ * HD), F32),
            shape_of((total, HD), F32),
            shape_of((total, HQ * HD)),
            shape_of((batches, WINDOW + rows, HD)),
            shape_of((batches, WINDOW + rows, HD)),
            shape_of((total // SUB, HQ * SUB, SPAN)),
            shape_of((total, HQ * HD)),
        ],
        compiler_params=pltpu.CompilerParams(
            vmem_limit_bytes=VMEM_LIMIT, dimension_semantics=("arbitrary", "arbitrary")
        ),
        cost_estimate=pl.CostEstimate(
            flops=flops, bytes_accessed=30 << 20, transcendentals=total * HQ * SPAN
        ),
        name="attention_forward",
    )(low, tokens, cos, sin, wq, wk, wv, g_pre, g_q, g_k)


def feed_forward(
    places, tokens, cotangent, context, wo, gate, up, down, g_attn, g_pre, g_post
):
    total, width = tokens.shape
    units = gate.shape[0]
    tile = lambda w: pl.BlockSpec((FF_TILE, w), lambda i: (i, 0))
    inner = context.shape[1]
    flops = 6 * total * width * (3 * units + inner)
    return pl.pallas_call(
        functools.partial(feed_forward_kernel, places),
        grid=(total // FF_TILE,),
        in_specs=[tile(width), tile(width), tile(inner)]
        + [whole(a.shape) for a in (wo, gate, up, down, g_attn, g_pre, g_post)],
        out_specs=[tile(width), tile(width), tile(inner), whole(wo.shape)]
        + [whole((units // 2, width))] * 6
        + [kept((1, width))] * 3,
        out_shape=[
            shape_of((total, width)),
            shape_of((total, width), F32),
            shape_of((total, inner)),
            shape_of(wo.shape),
        ]
        + [shape_of((units // 2, width))] * 6
        + [shape_of((1, width), F32)] * 3,
        scratch_shapes=[
            pltpu.VMEM((width, inner), F32),
            pltpu.VMEM((width, units), F32),
            pltpu.VMEM((width, units), F32),
            pltpu.VMEM((width, units), F32),
            pltpu.VMEM((FF_TILE, units), BF16),
            pltpu.VMEM((FF_TILE, units), F32),
            pltpu.VMEM((FF_TILE, units), F32),
        ],
        compiler_params=pltpu.CompilerParams(
            vmem_limit_bytes=VMEM_LIMIT, dimension_semantics=("arbitrary",)
        ),
        cost_estimate=pl.CostEstimate(
            flops=flops, bytes_accessed=40 << 20, transcendentals=total * units
        ),
        name="feed_forward",
    )(tokens, cotangent, context, wo, gate, up, down, g_attn, g_pre, g_post)


def attention_backward(
    tokens, d_middle, d_context, cos, sin, saved, wq, wk, wv, g_pre, g_q, g_k, batches
):
    total, width = tokens.shape
    rows = total // batches
    steps = rows // TILE
    back = lambda b, j: b * steps + steps - 1 - j
    tile = lambda w: pl.BlockSpec((TILE, w), lambda b, j: (back(b, j), 0))
    padded = pl.BlockSpec((1, WINDOW + rows, HD), lambda b, j: (b, 0, 0))
    subs = TILE // SUB
    columns = (HQ + 2) * HD
    flops = 2 * total * (width * columns * 2 + 4 * HQ * HD * SPAN)
    return pl.pallas_call(
        attention_backward_kernel,
        grid=(batches, steps),
        in_specs=[
            tile(width),
            tile(width),
            tile(HQ * HD),
            tile(HALF),
            tile(HALF),
            tile(HQ * HD),
            tile(HD),
            tile(HQ * HD),
            padded,
            padded,
            pl.BlockSpec((subs, HQ * SUB, SPAN), lambda b, j: (back(b, j), 0, 0)),
        ]
        + [whole(a.shape) for a in (wq, wk, wv, g_pre, g_q, g_k)],
        out_specs=[tile(width)]
        + [whole(a.shape) for a in (wq, wk, wv)]
        + [kept((1, width)), kept((1, HD)), kept((1, HD))],
        out_shape=[shape_of((total, width), F32)]
        + [shape_of(a.shape) for a in (wq, wk, wv)]
        + [shape_of((1, width), F32), shape_of((1, HD), F32), shape_of((1, HD), F32)],
        scratch_shapes=[
            pltpu.VMEM((width, columns), F32),
            pltpu.VMEM((HD, WINDOW + rows), F32),
            pltpu.VMEM((HD, WINDOW + rows), F32),
            pltpu.VMEM((TILE, columns), BF16),
        ],
        compiler_params=pltpu.CompilerParams(
            vmem_limit_bytes=VMEM_LIMIT, dimension_semantics=("arbitrary", "arbitrary")
        ),
        cost_estimate=pl.CostEstimate(flops=flops, bytes_accessed=45 << 20, transcendentals=0),
        name="attention_backward",
    )(tokens, d_middle, d_context, cos, sin, *saved, wq, wk, wv, g_pre, g_q, g_k)


def fold_kernel(count, last, *refs):
    keeps, arrived, outs = refs[:count], refs[count : 2 * count], refs[2 * count :]
    for i in range(count):
        half = keeps[i].shape[0] // 2
        if last:
            outs[i][...] = keeps[i][...].astype(F32) + arrived[i][...].astype(F32)
        else:
            for k, out in enumerate(outs[2 * i : 2 * i + 2]):
                rows = slice(k * half, (k + 1) * half)
                total = keeps[i][rows].astype(F32) + arrived[i][rows].astype(F32)
                out[...] = total.astype(BF16)


def fold(keeps, arrived, last):
    count = len(keeps)
    if last:
        out_shape = [shape_of(x.shape, F32) for x in keeps]
    else:
        out_shape = [shape_of((x.shape[0] // 2, x.shape[1])) for x in keeps for _ in range(2)]
    outs = pl.pallas_call(
        functools.partial(fold_kernel, count, last),
        grid=(1,),
        in_specs=[kept(x.shape) for x in (*keeps, *arrived)],
        out_specs=[kept(x.shape) for x in out_shape],
        out_shape=out_shape,
        compiler_params=pltpu.CompilerParams(vmem_limit_bytes=VMEM_LIMIT),
        cost_estimate=pl.CostEstimate(
            flops=sum(x.size for x in keeps),
            bytes_accessed=6 * sum(x.size for x in keeps),
            transcendentals=0,
        ),
        name="fold",
    )(*keeps, *arrived)
    return (outs, None) if last else (outs[0::2], outs[1::2])


def rows_layout(lengths, row_count):
    places = jnp.arange(row_count, dtype=jnp.int32)[None, :]
    ends = jnp.cumsum(lengths, axis=1)
    passed = places[:, :, None] >= ends[:, None, :]
    start = jnp.sum(jnp.where(passed, lengths[:, None, :], 0), axis=2)
    low = jnp.maximum(start, places - (WINDOW - 1)).reshape(-1, 1)
    frequency = jnp.exp(jnp.arange(HALF, dtype=F32) * (-2.0 * math.log(10000.0) / HD))
    angles = (places - start).astype(F32).reshape(-1, 1) * frequency[None, :]
    return low, jnp.cos(angles), jnp.sin(angles)


def swap(x, bit, count):
    return lax.ppermute(x, AXES, [(i, i ^ bit) for i in range(count)])


def bit_orders(count):
    bits = [1 << k for k in range(count.bit_length() - 1)]
    middle = bits[1:-1][::-1]
    orders = []
    for turn in range(3):
        turn %= max(len(middle), 1)
        orders.append([bits[-1]] + middle[turn:] + middle[:turn] + [bits[0]])
    return orders


def gather_relative(x, order, count):
    for bit in order:
        x = jnp.concatenate([x, swap(x, bit, count)], axis=0)
    return x


def gather_absolute(x, order, count, me):
    held = []
    for bit in order:
        other = swap(x, bit, count)
        mine_second = (me & bit) != 0
        axis = sum(1 for b in held if b > bit)
        x = jnp.stack(
            [jnp.where(mine_second, other, x), jnp.where(mine_second, x, other)], axis=axis
        )
        held.append(bit)
    return x.reshape((count,) + x.shape[len(order) :])


def places_of(order):
    count = 1 << len(order)
    return [sum(((m // bit) & 1) << k for k, bit in enumerate(order)) for m in range(count)]


def reorder(x, order_from, order_to, rows):
    n = len(order_from)
    y = x.reshape((2,) * n + (rows, x.shape[-1]))
    axes = [order_from[::-1].index(bit) for bit in order_to[::-1]]
    return y.transpose(axes + [n, n + 1]).reshape(x.shape)


def scatter_absolute(x, order, count, me):
    n = len(order)
    held = sorted(order)[::-1]
    x = x.reshape((2,) * n + x.shape[1:])
    for bit in order[::-1]:
        axis = held.index(bit)
        mine = ((me & bit) != 0).astype(jnp.int32)
        keep = lax.dynamic_index_in_dim(x, mine, axis, keepdims=False)
        send = lax.dynamic_index_in_dim(x, 1 - mine, axis, keepdims=False)
        held.remove(bit)
        total = keep.astype(F32) + swap(send, bit, count).astype(F32)
        x = total.astype(BF16) if bit != order[0] else total
    return x


def body(
    tokens,
    cotangent,
    lengths,
    w_query,
    w_key,
    w_value,
    w_out,
    w_gate,
    w_up,
    w_down,
    gain_pre_attn,
    gain_query,
    gain_key,
    gain_post_attn,
    gain_pre_ff,
    gain_post_ff,
):
    batches = lengths.shape[0]
    row_count = tokens.shape[0] // batches
    width = tokens.shape[1]
    count = lax.axis_size(AXES)
    me = lax.axis_index(AXES)
    orders = bit_orders(count)
    q_rows, k_rows, o_rows, f_rows = (
        w_query.shape[1],
        w_key.shape[1],
        w_out.shape[0],
        w_gate.shape[1],
    )
    flat = lambda gain: gain.reshape(1, -1)

    attn_shard = jnp.concatenate([w_query.T, w_key.T, w_value.T], axis=0)
    attn_all = gather_absolute(attn_shard, orders[0], count, me)
    full_query = attn_all[:, :q_rows].reshape(count * q_rows, width)
    full_key = attn_all[:, q_rows : q_rows + k_rows].reshape(count * k_rows, width)
    full_value = attn_all[:, q_rows + k_rows :].reshape(count * k_rows, width)
    full_out = gather_absolute(w_out, orders[1], count, me).reshape(count * o_rows, width)
    full_gate = gather_relative(w_gate.T, orders[0], count)
    full_up = reorder(gather_relative(w_up.T, orders[1], count), orders[1], orders[0], f_rows)
    full_down = reorder(gather_relative(w_down, orders[2], count), orders[2], orders[0], f_rows)

    low, cos, sin = rows_layout(lengths, row_count)
    *saved, context = attention_forward(
        tokens,
        low,
        cos,
        sin,
        full_query,
        full_key,
        full_value,
        flat(gain_pre_attn),
        flat(gain_query),
        flat(gain_key),
        batches,
    )
    turn_orders = [order[:-2] + [order[-1], order[-2]] for order in orders]
    first_places = places_of(orders[0])
    places = [
        [table[first_places.index(p)] for p in range(count)]
        for table in map(places_of, turn_orders)
    ]
    in_kernel = f_rows % 16 == 0
    if not in_kernel:
        places = [list(range(count))] * 3
    (
        result,
        d_middle,
        d_context,
        part_out,
        *ff,
        d_gain_post_attn,
        d_gain_pre_ff,
        d_gain_post_ff,
    ) = feed_forward(
        places if in_kernel else [[0, 1]] * 3,
        tokens,
        cotangent,
        context,
        full_out,
        full_gate,
        full_up,
        full_down,
        flat(gain_post_attn),
        flat(gain_pre_ff),
        flat(gain_post_ff),
    )
    keeps, sends = ff[0::2], ff[1::2]
    if not in_kernel:
        half = keeps[0].shape[0]
        ff = [
            reorder(jnp.concatenate([a, b]), orders[0], order, f_rows)
            for a, b, order in zip(keeps, sends, turn_orders)
        ]
        keeps, sends = [x[:half] for x in ff], [x[half:] for x in ff]
    turns = len(orders[0])

    def ff_turn(keeps, sends, k):
        arrived = [swap(x, order[-1 - k], count) for x, order in zip(sends, turn_orders)]
        return fold(keeps, arrived, k == turns - 1)

    (
        grad_source,
        part_query,
        part_key,
        part_value,
        d_gain_pre_attn,
        d_gain_query,
        d_gain_key,
    ) = attention_backward(
        tokens,
        d_middle,
        d_context,
        cos,
        sin,
        saved,
        full_query,
        full_key,
        full_value,
        flat(gain_pre_attn),
        flat(gain_query),
        flat(gain_key),
        batches,
    )
    arrived = [swap(x, order[-1], count) for x, order in zip(sends, turn_orders)]
    arrived, part_query = lax.optimization_barrier((arrived, part_query))
    keeps, sends = fold(keeps, arrived, turns == 1)
    done = 1
    grad_out = scatter_absolute(part_out.reshape(count, o_rows, width), orders[1], count, me)
    gains = (
        d_gain_pre_attn,
        d_gain_query,
        d_gain_key,
        d_gain_post_attn,
        d_gain_pre_ff,
        d_gain_post_ff,
    )
    total = jnp.concatenate(gains, axis=1).reshape(-1, 128)
    total = total + swap(total, 1, count)
    for k in range(done, turns):
        total, sends = lax.optimization_barrier((total, sends))
        total = total + swap(total, 1 << k, count)
        keeps, sends = ff_turn(keeps, sends, k)
    total = total.reshape(-1)
    grad_gate, grad_up, grad_down = keeps[0].T, keeps[1].T, keeps[2]
    attn_part = jnp.concatenate(
        [
            part_query.reshape(count, q_rows, width),
            part_key.reshape(count, k_rows, width),
            part_value.reshape(count, k_rows, width),
        ],
        axis=1,
    )
    attn_grad = scatter_absolute(attn_part, orders[0], count, me)
    grad_query = attn_grad[:q_rows].T
    grad_key = attn_grad[q_rows : q_rows + k_rows].T
    grad_value = attn_grad[q_rows + k_rows :].T

    gain_sums = []
    at = 0
    for gain in gains:
        gain_sums.append(total[at : at + gain.size])
        at += gain.size
    return (
        result,
        grad_source,
        grad_query,
        grad_key,
        grad_value,
        grad_out,
        grad_gate,
        grad_up,
        grad_down,
        *gain_sums,
    )


def solution(mesh):
    rows = P(("dp", "fsdp"), None)
    columns = P(None, ("dp", "fsdp"))
    return jax.shard_map(
        body,
        mesh=mesh,
        in_specs=(rows, rows, rows, columns, columns, columns, rows, columns, columns, rows)
        + (P(),) * 6,
        out_specs=(rows, rows, columns, columns, columns, rows, columns, columns, rows)
        + (P(),) * 6,
        check_vma=False,
    )
```

```python
import functools
import math

import jax
import jax.numpy as jnp
from jax import lax
from jax.experimental import pallas as pl
from jax.experimental.pallas import tpu as pltpu
from jax.sharding import PartitionSpec as P

HQ = 4
HD = 256
HALF = HD // 2
WINDOW = 512
AXES = ("dp", "fsdp")
EPS = 1e-06
SUB = 128
SPAN = WINDOW + SUB
TILE = 384
FF_TILE = 256
FF_CHUNK = 1024
VMEM_LIMIT = 60 * 1024 * 1024
F32 = jnp.float32
BF16 = jnp.bfloat16
GELU_C = math.sqrt(2.0 / math.pi)


def dot(left, right):
    return lax.dot_general(left, right, (((1,), (0,)), ((), ())), preferred_element_type=F32)


def dot_t(left, right):
    return lax.dot_general(left, right, (((1,), (1,)), ((), ())), preferred_element_type=F32)


def row_mean(v):
    return jnp.mean(v, axis=-1, keepdims=True)


def norm_scale(v):
    return lax.rsqrt(row_mean(v * v) + EPS)


def norm_back(v, gain, upstream):
    r = norm_scale(v)
    unit = v * r
    gu = gain * upstream
    dv = r * (gu - unit * row_mean(unit * gu))
    return dv, jnp.sum(upstream * unit, axis=0, keepdims=True)


def stack_heads(x):
    return jnp.concatenate([x[:, h * HD : (h + 1) * HD] for h in range(HQ)], axis=0)


def turn(v, cos, sin):
    a, b = v[:, :HALF], v[:, HALF:]
    return jnp.concatenate([a * cos - b * sin, b * cos + a * sin], axis=1)


def turn_back(v, cos, sin):
    a, b = v[:, :HALF], v[:, HALF:]
    return jnp.concatenate([a * cos + b * sin, b * cos - a * sin], axis=1)


def attention_forward_kernel(
    low_ref,
    tok_ref,
    cos_ref,
    sin_ref,
    wq_ref,
    wk_ref,
    wv_ref,
    g_pre_ref,
    g_q_ref,
    g_k_ref,
    qraw_ref,
    kraw_ref,
    q_ref,
    k_ref,
    v_ref,
    prob_ref,
    ctx_ref,
):
    j = pl.program_id(1)

    @pl.when(j == 0)
    def _():
        k_ref[0, :WINDOW] = jnp.zeros((WINDOW, HD), BF16)
        v_ref[0, :WINDOW] = jnp.zeros((WINDOW, HD), BF16)

    x = tok_ref[...].astype(F32)
    normed = (x * norm_scale(x) * g_pre_ref[...]).astype(BF16)
    cos, sin = cos_ref[...], sin_ref[...]
    key_raw = dot_t(normed, wk_ref[...])
    kraw_ref[...] = key_raw
    here = pl.ds(pl.multiple_of(WINDOW + j * TILE, 128), TILE)
    k_ref[0, here] = turn(key_raw * norm_scale(key_raw) * g_k_ref[...], cos, sin).astype(BF16)
    v_ref[0, here] = dot_t(normed, wv_ref[...]).astype(BF16)
    for h in range(HQ):
        cols = slice(h * HD, (h + 1) * HD)
        raw = dot_t(normed, wq_ref[cols])
        qraw_ref[:, cols] = raw
        q_ref[:, cols] = turn(raw * norm_scale(raw) * g_q_ref[...], cos, sin).astype(BF16)
    for s in range(TILE // SUB):
        rows = slice(s * SUB, (s + 1) * SUB)
        first = j * TILE + s * SUB
        window = pl.ds(pl.multiple_of(first, 128), SPAN)
        queries = stack_heads(q_ref[rows]) * jnp.asarray(HD**-0.5, BF16)
        scores = dot_t(queries, k_ref[0, window])
        column = lax.broadcasted_iota(jnp.int32, (SUB, SPAN), 1) + (first - WINDOW)
        row = lax.broadcasted_iota(jnp.int32, (SUB, SPAN), 0) + first
        visible = (column >= low_ref[rows]) & (column <= row)
        scores = jnp.where(visible[None], scores.reshape(HQ, SUB, SPAN), -1e30)
        exponent = jnp.exp(scores - jnp.max(scores, axis=-1, keepdims=True))
        share = 1.0 / jnp.sum(exponent, axis=-1, keepdims=True)
        prob = (exponent * share).astype(BF16).reshape(HQ * SUB, SPAN)
        prob_ref[s] = prob
        context = dot(prob, v_ref[0, window]).astype(BF16)
        for h in range(HQ):
            ctx_ref[rows, h * HD : (h + 1) * HD] = context[h * SUB : (h + 1) * SUB]


def feed_forward_kernel(
    places,
    tok_ref,
    cot_ref,
    ctx_ref,
    wo_ref,
    gate_ref,
    up_ref,
    down_ref,
    g_attn_ref,
    g_pre_ref,
    g_post_ref,
    out_ref,
    d_mid_ref,
    d_ctx_ref,
    p_out_ref,
    p_gate_keep,
    p_gate_send,
    p_up_keep,
    p_up_send,
    p_down_keep,
    p_down_send,
    d_g_attn_ref,
    d_g_pre_ref,
    d_g_post_ref,
    acc_out,
    acc_gate,
    acc_up,
    acc_down,
    hidden_sc,
    by_gate_sc,
    by_up_sc,
):
    step = pl.program_id(0)

    @pl.when(step == 0)
    def _():
        for ref in (acc_out, acc_gate, acc_up, acc_down, d_g_attn_ref, d_g_pre_ref, d_g_post_ref):
            ref[...] = jnp.zeros_like(ref)

    context = ctx_ref[...]
    branch = dot(context, wo_ref[...])
    middle = tok_ref[...].astype(F32) + branch * norm_scale(branch) * g_attn_ref[...]
    normed = (middle * norm_scale(middle) * g_pre_ref[...]).astype(BF16)
    units = gate_ref.shape[0]
    chunks = [slice(c, c + FF_CHUNK) for c in range(0, units, FF_CHUNK)]
    down_out = None
    for c in chunks:
        g = dot_t(normed, gate_ref[c])
        u = dot_t(normed, up_ref[c])
        g2 = g * g
        t = jnp.tanh(g * (GELU_C + (GELU_C * 0.044715) * g2))
        half = 0.5 * g
        gelu = half + half * t
        slope = (0.5 + 0.5 * t) + half * (1.0 - t * t) * (GELU_C + (3 * GELU_C * 0.044715) * g2)
        hidden = (gelu * u).astype(BF16)
        hidden_sc[:, c] = hidden
        by_gate_sc[:, c] = u * slope
        by_up_sc[:, c] = gelu
        part = dot(hidden, down_ref[c])
        down_out = part if down_out is None else down_out + part
    out_ref[...] = (middle + down_out * norm_scale(down_out) * g_post_ref[...]).astype(BF16)
    upstream = cot_ref[...].astype(F32)
    d_down, d_gain = norm_back(down_out, g_post_ref[...], upstream)
    d_g_post_ref[...] += d_gain
    d_down = d_down.astype(BF16)
    d_down_t = d_down.T
    normed_t = normed.T
    d_normed = None
    for c in chunks:
        d_hidden = dot_t(d_down, down_ref[c])
        d_gate = (d_hidden * by_gate_sc[:, c]).astype(BF16)
        d_up = (d_hidden * by_up_sc[:, c]).astype(BF16)
        acc_down[:, c] += dot(d_down_t, hidden_sc[:, c])
        acc_gate[:, c] += dot(normed_t, d_gate)
        acc_up[:, c] += dot(normed_t, d_up)
        part = dot(d_gate, gate_ref[c]) + dot(d_up, up_ref[c])
        d_normed = part if d_normed is None else d_normed + part
    d_middle, d_gain = norm_back(middle, g_pre_ref[...], d_normed)
    d_g_pre_ref[...] += d_gain
    d_middle = upstream + d_middle
    d_mid_ref[...] = d_middle
    d_branch, d_gain = norm_back(branch, g_attn_ref[...], d_middle)
    d_g_attn_ref[...] += d_gain
    d_branch = d_branch.astype(BF16)
    acc_out[...] += dot(d_branch.T, context)
    d_ctx_ref[...] = dot_t(d_branch, wo_ref[...]).astype(BF16)

    @pl.when(step == pl.num_programs(0) - 1)
    def _():
        for c in range(0, acc_out.shape[1], 256):
            p_out_ref[c : c + 256] = acc_out[:, c : c + 256].T.astype(BF16)
        blocks = len(places[0])
        size = acc_gate.shape[1] // blocks
        for acc, place, keep, send in (
            (acc_gate, places[0], p_gate_keep, p_gate_send),
            (acc_up, places[1], p_up_keep, p_up_send),
            (acc_down, places[2], p_down_keep, p_down_send),
        ):
            for c in range(0, acc.shape[1], 256):
                part = acc[:, c : c + 256].T.astype(BF16)
                for k in range(256 // size):
                    half, at = divmod(place[c // size + k], blocks // 2)
                    ref = send if half else keep
                    ref[at * size : (at + 1) * size] = part[k * size : (k + 1) * size]


def attention_backward_kernel(
    tok_ref,
    d_mid_ref,
    d_ctx_ref,
    cos_ref,
    sin_ref,
    qraw_ref,
    kraw_ref,
    q_ref,
    k_ref,
    v_ref,
    prob_ref,
    wq_ref,
    wk_ref,
    wv_ref,
    g_pre_ref,
    g_q_ref,
    g_k_ref,
    d_tok_ref,
    p_q_ref,
    p_k_ref,
    p_v_ref,
    d_g_pre_ref,
    d_g_q_ref,
    d_g_k_ref,
    acc,
    d_keys,
    d_values,
    d_raw,
):
    batch, step = pl.program_id(0), pl.program_id(1)
    j = pl.num_programs(1) - 1 - step
    qcols = HQ * HD
    scale = HD**-0.5

    @pl.when((batch == 0) & (step == 0))
    def _():
        for ref in (acc, d_g_pre_ref, d_g_q_ref, d_g_k_ref):
            ref[...] = jnp.zeros_like(ref)

    @pl.when(step == 0)
    def _():
        d_keys[...] = jnp.zeros_like(d_keys)
        d_values[...] = jnp.zeros_like(d_values)

    for s in range(TILE // SUB):
        rows = slice(s * SUB, (s + 1) * SUB)
        window = pl.ds(pl.multiple_of(j * TILE + s * SUB, 128), SPAN)
        d_context = stack_heads(d_ctx_ref[rows])
        queries = stack_heads(q_ref[rows])
        keys, values = k_ref[0, window], v_ref[0, window]
        prob = prob_ref[s]
        d_prob = dot_t(d_context, values)
        weight = prob.astype(F32)
        row_dot = jnp.sum(weight * d_prob, axis=-1, keepdims=True)
        d_scores = (weight * (d_prob - row_dot)).astype(BF16)
        d_queries = dot(d_scores, keys) * scale
        d_keys[:, window] += dot(queries.T, d_scores)
        d_values[:, window] += dot(d_context.T, prob)
        cos, sin = cos_ref[rows], sin_ref[rows]
        for h in range(HQ):
            cols = slice(h * HD, (h + 1) * HD)
            back = turn_back(d_queries[h * SUB : (h + 1) * SUB], cos, sin)
            d_q, d_gain = norm_back(qraw_ref[rows, cols], g_q_ref[...], back)
            d_g_q_ref[...] += d_gain
            d_raw[rows, cols] = d_q.astype(BF16)
    here = pl.ds(pl.multiple_of(WINDOW + j * TILE, 128), TILE)
    back = turn_back(d_keys[:, here].T * scale, cos_ref[...], sin_ref[...])
    d_k, d_gain = norm_back(kraw_ref[...], g_k_ref[...], back)
    d_g_k_ref[...] += d_gain
    d_raw[:, qcols : qcols + HD] = d_k.astype(BF16)
    d_raw[:, qcols + HD :] = d_values[:, here].T.astype(BF16)

    x = tok_ref[...].astype(F32)
    normed = (x * norm_scale(x) * g_pre_ref[...]).astype(BF16)
    normed_t = normed.T
    for c in range(0, qcols + 2 * HD, 512):
        acc[:, c : c + 512] += dot(normed_t, d_raw[:, c : c + 512])
    d_normed = (
        dot(d_raw[:, :qcols], wq_ref[...])
        + dot(d_raw[:, qcols : qcols + HD], wk_ref[...])
        + dot(d_raw[:, qcols + HD :], wv_ref[...])
    )
    d_x, d_gain = norm_back(x, g_pre_ref[...], d_normed)
    d_g_pre_ref[...] += d_gain
    d_tok_ref[...] = d_mid_ref[...] + d_x

    @pl.when((batch == pl.num_programs(0) - 1) & (step == pl.num_programs(1) - 1))
    def _():
        for h in range(HQ):
            cols = slice(h * HD, (h + 1) * HD)
            p_q_ref[cols] = acc[:, cols].T.astype(BF16)
        p_k_ref[...] = acc[:, qcols : qcols + HD].T.astype(BF16)
        p_v_ref[...] = acc[:, qcols + HD :].T.astype(BF16)


def whole(shape):
    return pl.BlockSpec(shape, lambda *_: (0,) * len(shape), pipeline_mode=pl.Buffered(1))


def kept(shape):
    return pl.BlockSpec(shape, lambda *_: (0,) * len(shape))


def shape_of(shape, dtype=BF16):
    return jax.ShapeDtypeStruct(shape, dtype)


def attention_forward(tokens, low, cos, sin, wq, wk, wv, g_pre, g_q, g_k, batches):
    total, width = tokens.shape
    rows = total // batches
    steps = rows // TILE
    tile = lambda w: pl.BlockSpec((TILE, w), lambda b, j: (b * steps + j, 0))
    padded = pl.BlockSpec((1, WINDOW + rows, HD), lambda b, j: (b, 0, 0))
    subs = TILE // SUB
    flops = 2 * total * (width * (HQ + 2) * HD + 2 * HQ * HD * SPAN)
    return pl.pallas_call(
        attention_forward_kernel,
        grid=(batches, steps),
        in_specs=[
            tile(1),
            tile(width),
            tile(HALF),
            tile(HALF),
            whole(wq.shape),
            whole(wk.shape),
            whole(wv.shape),
            whole(g_pre.shape),
            whole(g_q.shape),
            whole(g_k.shape),
        ],
        out_specs=[
            tile(HQ * HD),
            tile(HD),
            tile(HQ * HD),
            padded,
            padded,
            pl.BlockSpec((subs, HQ * SUB, SPAN), lambda b, j: (b * steps + j, 0, 0)),
            tile(HQ * HD),
        ],
        out_shape=[
            shape_of((total, HQ * HD), F32),
            shape_of((total, HD), F32),
            shape_of((total, HQ * HD)),
            shape_of((batches, WINDOW + rows, HD)),
            shape_of((batches, WINDOW + rows, HD)),
            shape_of((total // SUB, HQ * SUB, SPAN)),
            shape_of((total, HQ * HD)),
        ],
        compiler_params=pltpu.CompilerParams(
            vmem_limit_bytes=VMEM_LIMIT, dimension_semantics=("arbitrary", "arbitrary")
        ),
        cost_estimate=pl.CostEstimate(
            flops=flops, bytes_accessed=30 << 20, transcendentals=total * HQ * SPAN
        ),
        name="attention_forward",
    )(low, tokens, cos, sin, wq, wk, wv, g_pre, g_q, g_k)


def feed_forward(
    places, tokens, cotangent, context, wo, gate, up, down, g_attn, g_pre, g_post
):
    total, width = tokens.shape
    units = gate.shape[0]
    tile = lambda w: pl.BlockSpec((FF_TILE, w), lambda i: (i, 0))
    inner = context.shape[1]
    flops = 6 * total * width * (3 * units + inner)
    return pl.pallas_call(
        functools.partial(feed_forward_kernel, places),
        grid=(total // FF_TILE,),
        in_specs=[tile(width), tile(width), tile(inner)]
        + [whole(a.shape) for a in (wo, gate, up, down, g_attn, g_pre, g_post)],
        out_specs=[tile(width), tile(width), tile(inner), whole(wo.shape)]
        + [whole((units // 2, width))] * 6
        + [kept((1, width))] * 3,
        out_shape=[
            shape_of((total, width)),
            shape_of((total, width), F32),
            shape_of((total, inner)),
            shape_of(wo.shape),
        ]
        + [shape_of((units // 2, width))] * 6
        + [shape_of((1, width), F32)] * 3,
        scratch_shapes=[
            pltpu.VMEM((width, inner), F32),
            pltpu.VMEM((width, units), F32),
            pltpu.VMEM((width, units), F32),
            pltpu.VMEM((width, units), F32),
            pltpu.VMEM((FF_TILE, units), BF16),
            pltpu.VMEM((FF_TILE, units), F32),
            pltpu.VMEM((FF_TILE, units), F32),
        ],
        compiler_params=pltpu.CompilerParams(
            vmem_limit_bytes=VMEM_LIMIT, dimension_semantics=("arbitrary",)
        ),
        cost_estimate=pl.CostEstimate(
            flops=flops, bytes_accessed=40 << 20, transcendentals=total * units
        ),
        name="feed_forward",
    )(tokens, cotangent, context, wo, gate, up, down, g_attn, g_pre, g_post)


def attention_backward(
    tokens, d_middle, d_context, cos, sin, saved, wq, wk, wv, g_pre, g_q, g_k, batches
):
    total, width = tokens.shape
    rows = total // batches
    steps = rows // TILE
    back = lambda b, j: b * steps + steps - 1 - j
    tile = lambda w: pl.BlockSpec((TILE, w), lambda b, j: (back(b, j), 0))
    padded = pl.BlockSpec((1, WINDOW + rows, HD), lambda b, j: (b, 0, 0))
    subs = TILE // SUB
    columns = (HQ + 2) * HD
    flops = 2 * total * (width * columns * 2 + 4 * HQ * HD * SPAN)
    return pl.pallas_call(
        attention_backward_kernel,
        grid=(batches, steps),
        in_specs=[
            tile(width),
            tile(width),
            tile(HQ * HD),
            tile(HALF),
            tile(HALF),
            tile(HQ * HD),
            tile(HD),
            tile(HQ * HD),
            padded,
            padded,
            pl.BlockSpec((subs, HQ * SUB, SPAN), lambda b, j: (back(b, j), 0, 0)),
        ]
        + [whole(a.shape) for a in (wq, wk, wv, g_pre, g_q, g_k)],
        out_specs=[tile(width)]
        + [whole(a.shape) for a in (wq, wk, wv)]
        + [kept((1, width)), kept((1, HD)), kept((1, HD))],
        out_shape=[shape_of((total, width), F32)]
        + [shape_of(a.shape) for a in (wq, wk, wv)]
        + [shape_of((1, width), F32), shape_of((1, HD), F32), shape_of((1, HD), F32)],
        scratch_shapes=[
            pltpu.VMEM((width, columns), F32),
            pltpu.VMEM((HD, WINDOW + rows), F32),
            pltpu.VMEM((HD, WINDOW + rows), F32),
            pltpu.VMEM((TILE, columns), BF16),
        ],
        compiler_params=pltpu.CompilerParams(
            vmem_limit_bytes=VMEM_LIMIT, dimension_semantics=("arbitrary", "arbitrary")
        ),
        cost_estimate=pl.CostEstimate(flops=flops, bytes_accessed=45 << 20, transcendentals=0),
        name="attention_backward",
    )(tokens, d_middle, d_context, cos, sin, *saved, wq, wk, wv, g_pre, g_q, g_k)


def fold_kernel(count, last, *refs):
    keeps, arrived, outs = refs[:count], refs[count : 2 * count], refs[2 * count :]
    for i in range(count):
        half = keeps[i].shape[0] // 2
        if last:
            outs[i][...] = keeps[i][...].astype(F32) + arrived[i][...].astype(F32)
        else:
            for k, out in enumerate(outs[2 * i : 2 * i + 2]):
                rows = slice(k * half, (k + 1) * half)
                total = keeps[i][rows].astype(F32) + arrived[i][rows].astype(F32)
                out[...] = total.astype(BF16)


def fold(keeps, arrived, last):
    count = len(keeps)
    if last:
        out_shape = [shape_of(x.shape, F32) for x in keeps]
    else:
        out_shape = [shape_of((x.shape[0] // 2, x.shape[1])) for x in keeps for _ in range(2)]
    outs = pl.pallas_call(
        functools.partial(fold_kernel, count, last),
        grid=(1,),
        in_specs=[kept(x.shape) for x in (*keeps, *arrived)],
        out_specs=[kept(x.shape) for x in out_shape],
        out_shape=out_shape,
        compiler_params=pltpu.CompilerParams(vmem_limit_bytes=VMEM_LIMIT),
        cost_estimate=pl.CostEstimate(
            flops=sum(x.size for x in keeps),
            bytes_accessed=6 * sum(x.size for x in keeps),
            transcendentals=0,
        ),
        name="fold",
    )(*keeps, *arrived)
    return (outs, None) if last else (outs[0::2], outs[1::2])


def rows_layout(lengths, row_count):
    places = jnp.arange(row_count, dtype=jnp.int32)[None, :]
    ends = jnp.cumsum(lengths, axis=1)
    passed = places[:, :, None] >= ends[:, None, :]
    start = jnp.sum(jnp.where(passed, lengths[:, None, :], 0), axis=2)
    low = jnp.maximum(start, places - (WINDOW - 1)).reshape(-1, 1)
    frequency = jnp.exp(jnp.arange(HALF, dtype=F32) * (-2.0 * math.log(10000.0) / HD))
    angles = (places - start).astype(F32).reshape(-1, 1) * frequency[None, :]
    return low, jnp.cos(angles), jnp.sin(angles)


def swap(x, bit, count):
    return lax.ppermute(x, AXES, [(i, i ^ bit) for i in range(count)])


def bit_orders(count):
    bits = [1 << k for k in range(count.bit_length() - 1)]
    middle = bits[1:-1][::-1]
    orders = []
    for turn in range(3):
        turn %= max(len(middle), 1)
        orders.append([bits[-1]] + middle[turn:] + middle[:turn] + [bits[0]])
    return orders


def gather_relative(x, order, count):
    for bit in order:
        x = jnp.concatenate([x, swap(x, bit, count)], axis=0)
    return x


def gather_absolute(x, order, count, me):
    held = []
    for bit in order:
        other = swap(x, bit, count)
        mine_second = (me & bit) != 0
        axis = sum(1 for b in held if b > bit)
        x = jnp.stack(
            [jnp.where(mine_second, other, x), jnp.where(mine_second, x, other)], axis=axis
        )
        held.append(bit)
    return x.reshape((count,) + x.shape[len(order) :])


def places_of(order):
    count = 1 << len(order)
    return [sum(((m // bit) & 1) << k for k, bit in enumerate(order)) for m in range(count)]


def reorder(x, order_from, order_to, rows):
    n = len(order_from)
    y = x.reshape((2,) * n + (rows, x.shape[-1]))
    axes = [order_from[::-1].index(bit) for bit in order_to[::-1]]
    return y.transpose(axes + [n, n + 1]).reshape(x.shape)


def scatter_absolute(x, order, count, me):
    n = len(order)
    held = sorted(order)[::-1]
    x = x.reshape((2,) * n + x.shape[1:])
    for bit in order[::-1]:
        axis = held.index(bit)
        mine = ((me & bit) != 0).astype(jnp.int32)
        keep = lax.dynamic_index_in_dim(x, mine, axis, keepdims=False)
        send = lax.dynamic_index_in_dim(x, 1 - mine, axis, keepdims=False)
        held.remove(bit)
        total = keep.astype(F32) + swap(send, bit, count).astype(F32)
        x = total.astype(BF16) if bit != order[0] else total
    return x


def body(
    tokens,
    cotangent,
    lengths,
    w_query,
    w_key,
    w_value,
    w_out,
    w_gate,
    w_up,
    w_down,
    gain_pre_attn,
    gain_query,
    gain_key,
    gain_post_attn,
    gain_pre_ff,
    gain_post_ff,
):
    batches = lengths.shape[0]
    row_count = tokens.shape[0] // batches
    width = tokens.shape[1]
    count = lax.axis_size(AXES)
    me = lax.axis_index(AXES)
    orders = bit_orders(count)
    q_rows, k_rows, o_rows, f_rows = (
        w_query.shape[1],
        w_key.shape[1],
        w_out.shape[0],
        w_gate.shape[1],
    )
    turn_orders = [order[:-2] + [order[-1], order[-2]] for order in orders]
    flat = lambda gain: gain.reshape(1, -1)

    attn_shard = jnp.concatenate([w_query.T, w_key.T, w_value.T], axis=0)
    attn_all = gather_absolute(attn_shard, orders[0], count, me)
    full_query = attn_all[:, :q_rows].reshape(count * q_rows, width)
    full_key = attn_all[:, q_rows : q_rows + k_rows].reshape(count * k_rows, width)
    full_value = attn_all[:, q_rows + k_rows :].reshape(count * k_rows, width)
    full_out = gather_absolute(w_out, orders[1], count, me).reshape(count * o_rows, width)
    full_gate, full_up, full_down = (
        reorder(gather_relative(shard, order, count), order, turn_orders[0], f_rows)
        for shard, order in zip((w_gate.T, w_up.T, w_down), turn_orders)
    )

    low, cos, sin = rows_layout(lengths, row_count)
    *saved, context = attention_forward(
        tokens,
        low,
        cos,
        sin,
        full_query,
        full_key,
        full_value,
        flat(gain_pre_attn),
        flat(gain_query),
        flat(gain_key),
        batches,
    )
    first_places = places_of(turn_orders[0])
    places = [
        [table[first_places.index(p)] for p in range(count)]
        for table in map(places_of, turn_orders)
    ]
    in_kernel = f_rows % 16 == 0
    if not in_kernel:
        places = [list(range(count))] * 3
    (
        result,
        d_middle,
        d_context,
        part_out,
        *ff,
        d_gain_post_attn,
        d_gain_pre_ff,
        d_gain_post_ff,
    ) = feed_forward(
        places if in_kernel else [[0, 1]] * 3,
        tokens,
        cotangent,
        context,
        full_out,
        full_gate,
        full_up,
        full_down,
        flat(gain_post_attn),
        flat(gain_pre_ff),
        flat(gain_post_ff),
    )
    keeps, sends = ff[0::2], ff[1::2]
    if not in_kernel:
        half = keeps[0].shape[0]
        ff = [
            reorder(jnp.concatenate([a, b]), turn_orders[0], order, f_rows)
            for a, b, order in zip(keeps, sends, turn_orders)
        ]
        keeps, sends = [x[:half] for x in ff], [x[half:] for x in ff]
    turns = len(orders[0])

    def ff_turn(keeps, sends, k):
        arrived = [swap(x, order[-1 - k], count) for x, order in zip(sends, turn_orders)]
        return fold(keeps, arrived, k == turns - 1)

    (
        grad_source,
        part_query,
        part_key,
        part_value,
        d_gain_pre_attn,
        d_gain_query,
        d_gain_key,
    ) = attention_backward(
        tokens,
        d_middle,
        d_context,
        cos,
        sin,
        saved,
        full_query,
        full_key,
        full_value,
        flat(gain_pre_attn),
        flat(gain_query),
        flat(gain_key),
        batches,
    )
    arrived = [swap(x, order[-1], count) for x, order in zip(sends, turn_orders)]
    arrived, part_query = lax.optimization_barrier((arrived, part_query))
    keeps, sends = fold(keeps, arrived, turns == 1)
    done = 1
    grad_out = scatter_absolute(part_out.reshape(count, o_rows, width), orders[1], count, me)
    gains = (
        d_gain_pre_attn,
        d_gain_query,
        d_gain_key,
        d_gain_post_attn,
        d_gain_pre_ff,
        d_gain_post_ff,
    )
    total = jnp.concatenate(gains, axis=1).reshape(-1, 128)
    total = total + swap(total, 1, count)
    for k in range(done, turns):
        total, sends = lax.optimization_barrier((total, sends))
        total = total + swap(total, 1 << k, count)
        keeps, sends = ff_turn(keeps, sends, k)
    total = total.reshape(-1)
    grad_gate, grad_up, grad_down = keeps[0].T, keeps[1].T, keeps[2]
    attn_part = jnp.concatenate(
        [
            part_query.reshape(count, q_rows, width),
            part_key.reshape(count, k_rows, width),
            part_value.reshape(count, k_rows, width),
        ],
        axis=1,
    )
    attn_grad = scatter_absolute(attn_part, orders[0], count, me)
    grad_query = attn_grad[:q_rows].T
    grad_key = attn_grad[q_rows : q_rows + k_rows].T
    grad_value = attn_grad[q_rows + k_rows :].T

    gain_sums = []
    at = 0
    for gain in gains:
        gain_sums.append(total[at : at + gain.size])
        at += gain.size
    return (
        result,
        grad_source,
        grad_query,
        grad_key,
        grad_value,
        grad_out,
        grad_gate,
        grad_up,
        grad_down,
        *gain_sums,
    )


def solution(mesh):
    rows = P(("dp", "fsdp"), None)
    columns = P(None, ("dp", "fsdp"))
    return jax.shard_map(
        body,
        mesh=mesh,
        in_specs=(rows, rows, rows, columns, columns, columns, rows, columns, columns, rows)
        + (P(),) * 6,
        out_specs=(rows, rows, columns, columns, columns, rows, columns, columns, rows)
        + (P(),) * 6,
        check_vma=False,
    )
```
